512 devices in a mesh: dp: 16 (over y, x_hi, core), layer: 16 (over z), rep: 2 (over x_lo).
Axes of the slice: x: 4 (x_hi: 2, x_lo: 2; x = x_hi * 2 + x_lo), y: 4, z: 16, core: 2. Of those that a mesh axis runs over, the one named last changes fastest.
Arguments:
- grads: bfloat16 [4096, 40960], P('dp', 'layer'), may hold values from -4000 to 4000
Outputs:
- cosine: float32 [4096, 4096], P('dp', ('layer', 'rep'))
The draws below stay inside these ranges and needn't reach their ends.
All inputs are finite; a program needn't handle non-finite values.
Results may differ from the reference program's by a relative error of at most 0.0003.
Values may be sent and summed in bfloat16 or wider, within the bound.
A program may use at most 64 MiB of HBM per device.

```python
import math
import jax
import jax.numpy as jnp
from jax import lax

GROUP = 2560
EXAMPLES = 4096
FEATS = 40960


def draw_grads(key, part):
    key = jax.random.fold_in(key, 11)
    keys = jax.random.split(key, 7)
    labels = jax.random.randint(keys[0], (EXAMPLES,), 0, 32)
    centers = jnp.clip(jax.random.normal(keys[1], (32, FEATS), jnp.float32), -4.0, 4.0)
    weight_mix = jax.random.uniform(keys[2], (EXAMPLES, 1), jnp.float32, 0.3, 1.5)
    group_count = FEATS // GROUP
    ramp = jnp.sqrt(1.0 + 2.0 * (jnp.arange(FEATS) // GROUP).astype(jnp.float32) / max(group_count - 1, 1))
    feat_scale = jnp.exp(jax.random.uniform(keys[3], (1, FEATS), jnp.float32, 0.0, math.log(10.0))) * ramp[None, :]
    noise = jnp.clip(jax.random.normal(keys[4], (EXAMPLES, FEATS), jnp.float32), -4.0, 4.0)
    row_top = math.log(10.0)
    row_scale = jnp.exp(jax.random.uniform(keys[6], (EXAMPLES, 1), jnp.float32, 0.0, row_top))
    values = row_scale * feat_scale * (noise + weight_mix * centers[labels])
    return values.astype(jnp.bfloat16)


def setup_inputs(seed: int = 0) -> dict:
    splits = jax.random.split(jax.random.key(seed), 2)
    grads = draw_grads(jax.random.fold_in(splits[1], 71), 0)
    return dict(grads=grads)


def reference(grads):
    squares = lax.optimization_barrier(jnp.sum(jnp.square(grads.astype(jnp.float32)), axis=1))
    gram = jnp.dot(grads, grads.T, preferred_element_type=jnp.float32)
    inverse = lax.rsqrt(squares + 1e-06)
    return gram * inverse[:, None] * inverse[None, :]
```

```python
import functools

import jax
import jax.numpy as jnp
from jax import lax
from jax.experimental import pallas as pl
from jax.experimental.pallas import tpu as pltpu
from jax.sharding import PartitionSpec as P

MESH = pl.DeviceIdType.MESH
F32 = jnp.float32
BF16 = jnp.bfloat16
FEATURES = 2560
HALF = FEATURES // 2
CODE_SCALE = 32768.0
UP, DOWN, OUT, FAR, OWN, OWN0, OWN1 = range(7)
TILES = (
    (OWN, OWN),
    (OWN0, OWN1),
    (OWN, UP),
    (OWN, DOWN),
    (OWN, OUT),
    (UP, DOWN),
    (UP, OUT),
    (DOWN, OUT),
    (OWN, FAR),
)
TILE_COUNT = len(TILES)
NEAR = TILE_COUNT - 1


def edge_bit(h, y):
    return (h + (3 - y % 4) // 3) % 2


def is_direct(dp, layer, rep, half):
    yd, hd = dp // 4, (dp // 2) % 2
    yl, hl = layer // 4, (layer // 2) % 2
    dh, dy = (hl + hd) % 2, (yl - yd + 4) % 4
    parity = (hd + yd) % 2
    mixed = (half + rep) % 2
    above = edge_bit(hd, yd)
    second = edge_bit(hd, yd + 1)
    below = edge_bit(hd, yd + 3)
    same_column = jnp.where(
        dy == 0,
        jnp.where(mixed == 0, 0, half),
        jnp.where(
            dy == 1,
            (mixed + parity + above) % 2,
            jnp.where(dy == 3, (mixed + parity + below) % 2, (mixed + above + second + 1) % 2),
        ),
    )
    other_column = jnp.where(
        dy == 1,
        (mixed + above) % 2,
        jnp.where(dy == 3, (mixed + below) % 2, (mixed + parity) % 2),
    )
    return jnp.where(dh == 0, same_column, other_column) == 0


def decode(code):
    wide = code.astype(F32)
    size = jnp.abs(wide)
    quarter = lax.rsqrt(lax.rsqrt(jnp.maximum(size, 1e-37)))
    eighth = quarter * lax.rsqrt(quarter) * (1.0 / CODE_SCALE)
    return jnp.where(size < 1e-37, 0.0, jnp.where(wide < 0.0, -eighth, eighth))


def kernel(
    g_ref, out_ref, near, own, part, other, total, paired, code, codes, final, staging,
    squares, norm, near_norm, own_norm, row_scale,
    gather_send, gather_recv, own_send, own_recv, local_sem, far_sem, square_send, square_recv,
    norm_send, norm_recv, core_send, core_recv, pair_send, pair_recv, code_send, code_recv,
    final_send, final_recv,
):
    dp = lax.axis_index("dp")
    z = lax.axis_index("layer")
    r = lax.axis_index("rep")
    y, h, c = dp // 4, (dp // 2) % 2, dp % 2
    parity = (h + y) % 2
    g = (r + parity) % 2
    odd = z % 2

    def device(y_, h_, c_, z_, r_):
        return (4 * ((y_ + 4) % 4) + 2 * (h_ % 2) + c_, (z_ + 16) % 16, r_)

    def remote(src, dst, send, recv, target):
        return pltpu.make_async_remote_copy(
            src_ref=src, dst_ref=dst, send_sem=send, recv_sem=recv, device_id=target, device_id_type=MESH
        )

    barrier = pltpu.get_barrier_semaphore()
    partners = [device(y, h, 1 - c, z, r), device(y, h, c, z, 1 - r), device(y + 2, h, c, z, r)]
    for core in range(2):
        partners += [device(y + 1, h, core, z, r), device(y + 3, h, core, z, r), device(y, h + 1, core, z, 1 - r)]
    for target in partners:
        pl.semaphore_signal(barrier, inc=1, device_id=target, device_id_type=MESH)
    for step in range(1, 16):
        pl.semaphore_signal(barrier, inc=1, device_id=device(y, h, c, z + step, r), device_id_type=MESH)

    wide = g_ref[...].astype(F32)
    local = jnp.sum(wide * wide, axis=1, keepdims=True)
    squares[z] = jnp.broadcast_to(local, (256, 128)).T[0:1, :]

    pl.semaphore_wait(barrier, len(partners) + 15)

    sends = []
    wants = (
        (UP, (r + edge_bit(h, y + 3)) % 2, y + 3, h, r),
        (DOWN, (r + edge_bit(h, y)) % 2, y + 1, h, r),
        (OUT, 1 - r, y, h + 1, 1 - r),
    )
    for slot, half, y_, h_, r_ in wants:
        rows = pl.ds(pl.multiple_of(half * 128, 128), 128)
        for core in range(2):
            sends.append(
                remote(
                    g_ref.at[rows, pl.ds(core * HALF, HALF)],
                    near.at[slot, pl.ds(pl.multiple_of(c * 128, 128), 128)],
                    gather_send.at[slot, core],
                    gather_recv.at[slot, c],
                    device(y_, h_, core, z, r_),
                )
            )
    for copy in sends:
        copy.start()
    square_sends = []
    for step in range(1, 16):
        square_sends.append(
            remote(
                squares.at[z], squares.at[z], square_send.at[step], square_recv.at[z],
                device(y, h, c, z + step, r),
            )
        )
        square_sends[-1].start()
    mine = pl.ds(pl.multiple_of(c * HALF, 128), HALF)
    theirs = pl.ds(pl.multiple_of((1 - c) * HALF, 128), HALF)
    place = pl.ds(pl.multiple_of(c * 128, 128), 128)
    own_sends = []
    own_copies = []
    for half in range(2):
        rows = pl.ds(half * 128, 128)
        own_sends.append(
            remote(
                g_ref.at[rows, theirs], own.at[half, place], own_send.at[half], own_recv.at[half],
                device(y, h, 1 - c, z, r),
            )
        )
        own_copies.append(pltpu.make_async_copy(g_ref.at[rows, mine], own.at[half, place], local_sem.at[half]))
    for copy in own_sends + own_copies:
        copy.start()

    for step in range(1, 16):
        source = (z + step) % 16
        remote(
            squares.at[source], squares.at[source], square_send.at[step], square_recv.at[source],
            device(y, h, c, z + step, r),
        ).wait_recv()
    inverse = lax.rsqrt(jnp.sum(squares[...], axis=0) + 1e-06)
    norm[0] = inverse[:, 0:128]
    norm[1] = inverse[:, 128:256]
    norm_sends = []
    for slot, half, y_, h_, r_ in wants:
        for core in range(2):
            norm_sends.append(
                remote(
                    norm.at[half], near_norm.at[slot, c], norm_send.at[slot, core], norm_recv.at[slot, c],
                    device(y_, h_, core, z, r_),
                )
            )
    for half in range(2):
        own_norm[half, c] = norm[half]
        norm_sends.append(
            remote(
                norm.at[half], own_norm.at[half, c], norm_send.at[4, half], norm_recv.at[4, half],
                device(y, h, 1 - c, z, r),
            )
        )
    for copy in norm_sends:
        copy.start()

    def block(kind):
        if kind == OWN:
            return own[g]
        if kind in (OWN0, OWN1):
            return own[kind - OWN0]
        return near[kind]

    def norms(kind, index):
        if kind == OWN:
            return own_norm[g, index]
        if kind in (OWN0, OWN1):
            return own_norm[kind - OWN0, index]
        return near_norm[kind, index]

    core_sends = []

    def product(tile):
        left, right = TILES[tile]
        value = lax.dot_general(block(left), block(right), (((1,), (1,)), ((), ())), preferred_element_type=F32)
        part[tile, 0] = value[:, 0:128]
        part[tile, 1] = value[:, 128:256]
        core_sends.append(
            remote(
                part.at[tile, 1 - c], other.at[tile], core_send.at[tile], core_recv.at[tile],
                device(y, h, 1 - c, z, r),
            )
        )
        core_sends[-1].start()

    for half in range(2):
        own_copies[half].wait()
        own_sends[half].wait_recv()
    product(0)
    product(1)

    def arrived(slot):
        for core in range(2):
            remote(
                near.at[slot, pl.ds(core * 128, 128)], near.at[slot, pl.ds(core * 128, 128)],
                gather_send.at[slot, core], gather_recv.at[slot, core], device(y, h, 1 - c, z, r),
            ).wait_recv()
            remote(
                near_norm.at[slot, core], near_norm.at[slot, core],
                norm_send.at[slot, core], norm_recv.at[slot, core], device(y, h, 1 - c, z, r),
            ).wait_recv()

    arrived(OUT)
    far_copy = remote(near.at[OUT], near.at[FAR], far_sem.at[0], far_sem.at[1], device(y + 2, h, c, z, r))
    far_copy.start()
    far_norm = remote(near_norm.at[OUT], near_norm.at[FAR], far_sem.at[2], far_sem.at[3], device(y + 2, h, c, z, r))
    far_norm.start()
    arrived(UP)
    arrived(DOWN)
    for half in range(2):
        remote(
            own_norm.at[half, 1 - c], own_norm.at[half, 1 - c], norm_send.at[4, half], norm_recv.at[4, half],
            device(y, h, 1 - c, z, r),
        ).wait_recv()
    for tile in range(2, NEAR):
        product(tile)

    scale_slot = {OWN: 0, OWN0: 1, UP: 2, DOWN: 3}
    for kind, index in scale_slot.items():
        for half in range(2):
            square = jnp.broadcast_to(norms(kind, half), (128, 128)).T * CODE_SCALE
            row_scale[index, 2 * half] = square[0:64]
            row_scale[index, 2 * half + 1] = square[64:128]

    pair_targets = (device(y, h, c, z + 1 - 2 * odd, r), device(y, h, c, z - 1 + 2 * odd, r))

    def pair_copies(first, count, batch):
        copies = []
        for side in range(2):
            copies.append(
                remote(
                    total.at[pl.ds(first, count), 2 * side + 1 - odd], paired.at[side, pl.ds(first, count)],
                    pair_send.at[batch, side], pair_recv.at[batch, side], pair_targets[side],
                )
            )
        return copies

    def join_cores(tile):
        core_sends[tile].wait_recv()
        value = part[tile, c] + other[tile]
        for quarter in range(4):
            total[tile, quarter] = value[64 * quarter : 64 * quarter + 64]

    def encode_tile(tile):
        left, right = TILES[tile]
        columns = norms(right, c)
        for side in range(2):
            quarter = 2 * side + odd
            value = total[tile, quarter] + paired[side, tile]
            scaled = value * row_scale[scale_slot[left], quarter] * columns
            square = scaled * scaled
            coded = (square * square * square * scaled * jnp.abs(scaled)).astype(BF16)
            for j in range(4):
                code[2 * j + side, tile] = coded[16 * j : 16 * j + 16]

    def code_copies(first, count, batch):
        copies = []
        for step in range(1, 8):
            slot = (z // 2 + step) % 8
            copies.append(
                remote(
                    code.at[slot, pl.ds(first, count)], codes.at[z // 2, pl.ds(first, count)],
                    code_send.at[batch, step], code_recv.at[batch, z // 2],
                    device(y, h, c, 2 * slot + odd, r),
                )
            )
        return copies

    def wait_codes(first, count, batch):
        for step in range(1, 8):
            slot = (z // 2 + step) % 8
            remote(
                codes.at[slot, pl.ds(first, count)], codes.at[slot, pl.ds(first, count)],
                code_send.at[batch, step], code_recv.at[batch, slot],
                device(y, h, c, 2 * slot + odd, r),
            ).wait_recv()

    def sum_codes(first, count):
        value = decode(code[z // 2, first : first + count])
        for step in range(1, 8):
            value = value + decode(codes[(z // 2 + step) % 8, first : first + count])
        final[first : first + count] = value

    row_block = (z % 4) // 2
    offset = pl.multiple_of(64 * (z % 2) + 16 * (z // 4), 16)
    strip = pl.ds(offset, 16)
    sets = {
        OWN: (y, h, g),
        OWN0: (y, h, 0),
        OWN1: (y, h, 1),
        UP: (y + 1, h, (r + edge_bit(h, y)) % 2),
        DOWN: (y + 3, h, (r + edge_bit(h, y + 3)) % 2),
        OUT: (y, h + 1, r),
        FAR: (y + 2, h + 1, r),
    }

    def index_of(kind, block_index):
        y_, h_, _ = sets[kind]
        return 4 * ((y_ + 4) % 4) + 2 * (h_ % 2) + block_index

    final_waits = []

    def deliver(tile, number, row, column, rep, half):
        copy = remote(
            final.at[tile], staging.at[half, strip], final_send.at[tile, number], final_recv, (row, column, rep)
        )
        here = jnp.logical_and(jnp.logical_and(row == dp, column == z), rep == r)
        stay = pltpu.make_async_copy(final.at[tile], staging.at[half, strip], final_recv)

        @pl.when(jnp.logical_not(here))
        def _():
            copy.start()

        @pl.when(here)
        def _():
            stay.start()

        final_waits.append((copy, here))

    def deliver_tile(tile):
        left, right = TILES[tile]
        row, column = index_of(left, row_block), index_of(right, c)
        left_set, right_set = sets[left][2], sets[right][2]
        if tile == 0:
            deliver(tile, 0, row, column, right_set, left_set)
        elif tile == 1:
            first = r == 0
            deliver(
                tile, 0, jnp.where(first, row, column), jnp.where(first, column, row),
                jnp.where(first, 1, 0), jnp.where(first, 0, 1),
            )
        else:
            deliver(tile, 0, row, column, right_set, left_set)
            deliver(tile, 1, column, row, left_set, right_set)

    for tile in range(NEAR):
        join_cores(tile)
    pair_first = pair_copies(0, NEAR, 0)
    for copy in pair_first:
        copy.start()
    for copy in pair_first:
        copy.wait_recv()
    for tile in range(NEAR):
        encode_tile(tile)
    codes_first = code_copies(0, NEAR, 0)
    for copy in codes_first:
        copy.start()

    far_copy.wait_recv()
    far_norm.wait_recv()
    product(NEAR)
    join_cores(NEAR)
    pair_second = pair_copies(NEAR, 1, 1)
    for copy in pair_second:
        copy.start()
    for copy in pair_second:
        copy.wait_recv()
    encode_tile(NEAR)
    codes_second = code_copies(NEAR, 1, 1)
    for copy in codes_second:
        copy.start()

    wait_codes(0, NEAR, 0)
    sum_codes(0, NEAR)
    for tile in range(NEAR):
        deliver_tile(tile)
    wait_codes(NEAR, 1, 1)
    sum_codes(NEAR, 1)
    deliver_tile(NEAR)

    pltpu.make_async_copy(staging, staging, final_recv).wait()
    for half in range(2):
        direct = is_direct(dp, z, r, half)

        @pl.when(direct)
        def _():
            out_ref[pl.ds(half * 128, 128), :] = staging[half]

        @pl.when(jnp.logical_not(direct))
        def _():
            out_ref[pl.ds(half * 128, 128), :] = staging[half].T

    waits = sends + square_sends + own_sends + norm_sends + [far_copy, far_norm] + core_sends
    waits += pair_first + pair_second + codes_first + codes_second
    for copy in waits:
        copy.wait_send()
    for copy, here in final_waits:

        @pl.when(jnp.logical_not(here))
        def _():
            copy.wait_send()


def body(grads):
    dma = pltpu.SemaphoreType.DMA
    return pl.pallas_call(
        kernel,
        out_shape=jax.ShapeDtypeStruct((256, 128), F32),
        in_specs=[pl.BlockSpec(memory_space=pltpu.VMEM)],
        out_specs=pl.BlockSpec(memory_space=pltpu.VMEM),
        scratch_shapes=[
            pltpu.VMEM((4, 256, HALF), BF16),
            pltpu.VMEM((2, 256, HALF), BF16),
            pltpu.VMEM((TILE_COUNT, 2, 256, 128), F32),
            pltpu.VMEM((TILE_COUNT, 256, 128), F32),
            pltpu.VMEM((TILE_COUNT, 4, 64, 128), F32),
            pltpu.VMEM((2, TILE_COUNT, 64, 128), F32),
            pltpu.VMEM((8, TILE_COUNT, 16, 128), BF16),
            pltpu.VMEM((8, TILE_COUNT, 16, 128), BF16),
            pltpu.VMEM((TILE_COUNT, 16, 128), F32),
            pltpu.VMEM((2, 128, 128), F32),
            pltpu.VMEM((16, 1, 256), F32),
            pltpu.VMEM((2, 1, 128), F32),
            pltpu.VMEM((4, 2, 1, 128), F32),
            pltpu.VMEM((2, 2, 1, 128), F32),
            pltpu.VMEM((4, 4, 64, 128), F32),
            dma((3, 2)),
            dma((3, 2)),
            dma((2,)),
            dma((2,)),
            dma((2,)),
            dma((4,)),
            dma((16,)),
            dma((16,)),
            dma((5, 2)),
            dma((5, 2)),
            dma((TILE_COUNT,)),
            dma((TILE_COUNT,)),
            dma((2, 2)),
            dma((2, 2)),
            dma((2, 8)),
            dma((2, 8)),
            dma((TILE_COUNT, 2)),
            dma,
        ],
        compiler_params=pltpu.CompilerParams(
            collective_id=0, has_side_effects=True, vmem_limit_bytes=40 * 1024 * 1024
        ),
        cost_estimate=pl.CostEstimate(flops=1510000000, bytes_accessed=1500000, transcendentals=0),
    )(grads)


def solution(mesh):
    in_specs = (P("dp", "layer"),)
    out_specs = P("dp", ("layer", "rep"))
    return jax.shard_map(body, mesh=mesh, in_specs=in_specs, out_specs=out_specs, check_vma=False)
```

```python
import functools

import jax
import jax.numpy as jnp
from jax import lax
from jax.experimental import pallas as pl
from jax.experimental.pallas import tpu as pltpu
from jax.sharding import PartitionSpec as P

MESH = pl.DeviceIdType.MESH
F32 = jnp.float32
BF16 = jnp.bfloat16
FEATURES = 2560
HALF = FEATURES // 2
CODE_SCALE = 32768.0
UP, DOWN, OUT, FAR, OWN, OWN0, OWN1, LAST = range(8)
TILES = (
    (OWN, OWN),
    (OWN0, OWN1),
    (OWN, UP),
    (OWN, DOWN),
    (UP, DOWN),
    (UP, OUT),
    (DOWN, OUT),
    (OWN0, LAST),
    (OWN1, LAST),
)
TILE_COUNT = len(TILES)
BATCHES = ((0, 2), (2, 5), (7, 2))


def edge_bit(h, y):
    return (h + (3 - y % 4) // 3) % 2


def is_direct(dp, layer, rep, half):
    yd, hd = dp // 4, (dp // 2) % 2
    yl, hl = layer // 4, (layer // 2) % 2
    dh, dy = (hl + hd) % 2, (yl - yd + 4) % 4
    parity = (hd + yd) % 2
    mixed = (half + rep) % 2
    above = edge_bit(hd, yd)
    second = edge_bit(hd, yd + 1)
    below = edge_bit(hd, yd + 3)
    same_column = jnp.where(
        dy == 0,
        jnp.where(mixed == 0, 0, half),
        jnp.where(
            dy == 1,
            (mixed + parity + above) % 2,
            jnp.where(dy == 3, (mixed + parity + below) % 2, (mixed + above + second + 1) % 2),
        ),
    )
    other_column = jnp.where(
        dy == 1,
        (mixed + above) % 2,
        jnp.where(dy == 3, (mixed + below) % 2, jnp.where(dy == 0, 1 - parity, parity)),
    )
    return jnp.where(dh == 0, same_column, other_column) == 0


def decode(code):
    wide = code.astype(F32)
    size = jnp.abs(wide)
    quarter = lax.rsqrt(lax.rsqrt(jnp.maximum(size, 1e-37)))
    eighth = quarter * lax.rsqrt(quarter) * (1.0 / CODE_SCALE)
    return jnp.where(size < 1e-37, 0.0, jnp.where(wide < 0.0, -eighth, eighth))


def kernel(
    g_ref, out_ref, near, own, part, other, total, paired, code, codes, final, staging,
    squares, norm, near_norm, own_norm, row_scale,
    gather_send, gather_recv, own_send, own_recv, local_sem, far_sem, square_send, square_recv,
    norm_send, norm_recv, core_send, core_recv, pair_send, pair_recv, code_send, code_recv,
    final_send, final_recv,
):
    dp = lax.axis_index("dp")
    z = lax.axis_index("layer")
    r = lax.axis_index("rep")
    y, h, c = dp // 4, (dp // 2) % 2, dp % 2
    parity = (h + y) % 2
    g = (r + parity) % 2
    odd = z % 2
    even_chip = parity == 0
    last_slot = OUT + 1 - parity

    def device(y_, h_, c_, z_, r_):
        return (4 * ((y_ + 4) % 4) + 2 * (h_ % 2) + c_, (z_ + 16) % 16, r_)

    def remote(src, dst, send, recv, target):
        return pltpu.make_async_remote_copy(
            src_ref=src, dst_ref=dst, send_sem=send, recv_sem=recv, device_id=target, device_id_type=MESH
        )

    barrier = pltpu.get_barrier_semaphore()
    partners = [device(y, h, 1 - c, z, r), device(y, h, c, z, 1 - r), device(y + 2, h, c, z, r)]
    for core in range(2):
        partners += [device(y + 1, h, core, z, r), device(y + 3, h, core, z, r), device(y, h + 1, core, z, 1 - r)]
    for target in partners:
        pl.semaphore_signal(barrier, inc=1, device_id=target, device_id_type=MESH)
    for step in range(1, 16):
        pl.semaphore_signal(barrier, inc=1, device_id=device(y, h, c, z + step, r), device_id_type=MESH)

    wide = g_ref[...].astype(F32)
    local = jnp.sum(wide * wide, axis=1, keepdims=True)
    squares[z] = jnp.broadcast_to(local, (256, 128)).T[0:1, :]

    pl.semaphore_wait(barrier, len(partners) + 15)

    sends = []
    wants = (
        (UP, (r + edge_bit(h, y + 3)) % 2, y + 3, h, r),
        (DOWN, (r + edge_bit(h, y)) % 2, y + 1, h, r),
        (OUT, 1 - r, y, h + 1, 1 - r),
    )
    for slot, half, y_, h_, r_ in wants:
        rows = pl.ds(pl.multiple_of(half * 128, 128), 128)
        for core in range(2):
            sends.append(
                remote(
                    g_ref.at[rows, pl.ds(core * HALF, HALF)],
                    near.at[slot, pl.ds(pl.multiple_of(c * 128, 128), 128)],
                    gather_send.at[slot, core],
                    gather_recv.at[slot, c],
                    device(y_, h_, core, z, r_),
                )
            )
    for copy in sends:
        copy.start()
    square_sends = []
    for step in range(1, 16):
        square_sends.append(
            remote(
                squares.at[z], squares.at[z], square_send.at[step], square_recv.at[z],
                device(y, h, c, z + step, r),
            )
        )
        square_sends[-1].start()
    mine = pl.ds(pl.multiple_of(c * HALF, 128), HALF)
    theirs = pl.ds(pl.multiple_of((1 - c) * HALF, 128), HALF)
    place = pl.ds(pl.multiple_of(c * 128, 128), 128)
    own_sends = []
    own_copies = []
    for half in range(2):
        rows = pl.ds(half * 128, 128)
        own_sends.append(
            remote(
                g_ref.at[rows, theirs], own.at[half, place], own_send.at[half], own_recv.at[half],
                device(y, h, 1 - c, z, r),
            )
        )
        own_copies.append(pltpu.make_async_copy(g_ref.at[rows, mine], own.at[half, place], local_sem.at[half]))
    for copy in own_sends + own_copies:
        copy.start()

    def block(kind):
        if kind == OWN:
            return own[g]
        if kind in (OWN0, OWN1):
            return own[kind - OWN0]
        if kind == LAST:
            return near[last_slot]
        return near[kind]

    def norms(kind, index):
        if kind == OWN:
            return own_norm[g, index]
        if kind in (OWN0, OWN1):
            return own_norm[kind - OWN0, index]
        if kind == LAST:
            return near_norm[last_slot, index]
        return near_norm[kind, index]

    core_sends = []

    def product(tile):
        left, right = TILES[tile]
        value = lax.dot_general(block(left), block(right), (((1,), (1,)), ((), ())), preferred_element_type=F32)
        part[tile, 0] = value[:, 0:128]
        part[tile, 1] = value[:, 128:256]
        core_sends.append(
            remote(
                part.at[tile, 1 - c], other.at[tile], core_send.at[tile], core_recv.at[tile],
                device(y, h, 1 - c, z, r),
            )
        )
        core_sends[-1].start()

    def join_cores(tile):
        core_sends[tile].wait_recv()
        value = part[tile, c] + other[tile]
        for quarter in range(4):
            total[tile, quarter] = value[64 * quarter : 64 * quarter + 64]

    scale_slot = {OWN: 0, OWN0: 1, OWN1: 2, UP: 3, DOWN: 4}

    def spread_norms(kind):
        for half in range(2):
            square = jnp.broadcast_to(norms(kind, half), (128, 128)).T * CODE_SCALE
            row_scale[scale_slot[kind], 2 * half] = square[0:64]
            row_scale[scale_slot[kind], 2 * half + 1] = square[64:128]

    pair_targets = (device(y, h, c, z + 1 - 2 * odd, r), device(y, h, c, z - 1 + 2 * odd, r))

    def pair_copies(batch):
        first, count = BATCHES[batch]
        return [
            remote(
                total.at[pl.ds(first, count), 2 * side + 1 - odd], paired.at[side, pl.ds(first, count)],
                pair_send.at[batch, side], pair_recv.at[batch, side], pair_targets[side],
            )
            for side in range(2)
        ]

    def encode_tile(tile):
        left, right = TILES[tile]
        columns = norms(right, c)
        for side in range(2):
            quarter = 2 * side + odd
            value = total[tile, quarter] + paired[side, tile]
            scaled = value * row_scale[scale_slot[left], quarter] * columns
            square = scaled * scaled
            coded = (square * square * square * scaled * jnp.abs(scaled)).astype(BF16)
            for j in range(4):
                code[2 * j + side, tile] = coded[16 * j : 16 * j + 16]

    def code_copies(batch):
        first, count = BATCHES[batch]
        copies = []
        for step in range(1, 8):
            slot = (z // 2 + step) % 8
            copies.append(
                remote(
                    code.at[slot, pl.ds(first, count)], codes.at[z // 2, pl.ds(first, count)],
                    code_send.at[batch, step], code_recv.at[batch, z // 2],
                    device(y, h, c, 2 * slot + odd, r),
                )
            )
        return copies

    def wait_codes(batch):
        first, count = BATCHES[batch]
        for step in range(1, 8):
            slot = (z // 2 + step) % 8
            remote(
                codes.at[slot, pl.ds(first, count)], codes.at[slot, pl.ds(first, count)],
                code_send.at[batch, step], code_recv.at[batch, slot],
                device(y, h, c, 2 * slot + odd, r),
            ).wait_recv()

    def sum_codes(batch):
        first, count = BATCHES[batch]
        value = decode(code[z // 2, first : first + count])
        for step in range(1, 8):
            value = value + decode(codes[(z // 2 + step) % 8, first : first + count])
        final[first : first + count] = value

    row_block = (z % 4) // 2
    offset = pl.multiple_of(64 * (z % 2) + 16 * (z // 4), 16)
    strip = pl.ds(offset, 16)
    sets = {
        OWN: (y, h, g),
        OWN0: (y, h, 0),
        OWN1: (y, h, 1),
        UP: (y + 1, h, (r + edge_bit(h, y)) % 2),
        DOWN: (y + 3, h, (r + edge_bit(h, y + 3)) % 2),
        OUT: (y, h + 1, r),
        LAST: (y + 2 * (1 - parity), h + 1, r),
    }

    def index_of(kind, block_index):
        y_, h_, _ = sets[kind]
        return 4 * ((y_ + 4) % 4) + 2 * (h_ % 2) + block_index

    final_waits = []

    def deliver(tile, number, row, column, rep, half):
        copy = remote(
            final.at[tile], staging.at[half, strip], final_send.at[tile, number], final_recv, (row, column, rep)
        )
        here = jnp.logical_and(jnp.logical_and(row == dp, column == z), rep == r)
        stay = pltpu.make_async_copy(final.at[tile], staging.at[half, strip], final_recv)

        @pl.when(jnp.logical_not(here))
        def _():
            copy.start()

        @pl.when(here)
        def _():
            stay.start()

        final_waits.append((copy, here))

    def deliver_tile(tile):
        left, right = TILES[tile]
        row, column = index_of(left, row_block), index_of(right, c)
        left_set, right_set = sets[left][2], sets[right][2]
        if tile == 0:
            deliver(tile, 0, row, column, right_set, left_set)
        elif tile == 1:
            first = r == 0
            deliver(
                tile, 0, jnp.where(first, row, column), jnp.where(first, column, row),
                jnp.where(first, 1, 0), jnp.where(first, 0, 1),
            )
        else:
            deliver(tile, 0, row, column, right_set, left_set)
            deliver(tile, 1, column, row, left_set, right_set)

    def tiles_of(batch):
        first, count = BATCHES[batch]
        return range(first, first + count)

    def finish_batch(batch):
        wait_codes(batch)
        sum_codes(batch)
        for tile in tiles_of(batch):
            deliver_tile(tile)

    pairs = [pair_copies(batch) for batch in range(3)]
    code_sends = [code_copies(batch) for batch in range(3)]

    def start_pairs(batch):
        for tile in tiles_of(batch):
            join_cores(tile)
        for copy in pairs[batch]:
            copy.start()

    def start_codes(batch):
        for copy in pairs[batch]:
            copy.wait_recv()
        for tile in tiles_of(batch):
            encode_tile(tile)
        for copy in code_sends[batch]:
            copy.start()

    for half in range(2):
        own_copies[half].wait()
        own_sends[half].wait_recv()
    for tile in tiles_of(0):
        product(tile)

    for step in range(1, 16):
        source = (z + step) % 16
        remote(
            squares.at[source], squares.at[source], square_send.at[step], square_recv.at[source],
            device(y, h, c, z + step, r),
        ).wait_recv()
    inverse = lax.rsqrt(jnp.sum(squares[...], axis=0) + 1e-06)
    norm[0] = inverse[:, 0:128]
    norm[1] = inverse[:, 128:256]
    norm_sends = []
    for slot, half, y_, h_, r_ in wants:
        for core in range(2):
            norm_sends.append(
                remote(
                    norm.at[half], near_norm.at[slot, c], norm_send.at[slot, core], norm_recv.at[slot, c],
                    device(y_, h_, core, z, r_),
                )
            )
    for half in range(2):
        own_norm[half, c] = norm[half]
        norm_sends.append(
            remote(
                norm.at[half], own_norm.at[half, c], norm_send.at[4, half], norm_recv.at[4, half],
                device(y, h, 1 - c, z, r),
            )
        )
    for copy in norm_sends:
        copy.start()

    start_pairs(0)
    for half in range(2):
        remote(
            own_norm.at[half, 1 - c], own_norm.at[half, 1 - c], norm_send.at[4, half], norm_recv.at[4, half],
            device(y, h, 1 - c, z, r),
        ).wait_recv()
    for kind in (OWN, OWN0, OWN1):
        spread_norms(kind)
    start_codes(0)

    def arrived(slot):
        for core in range(2):
            remote(
                near_norm.at[slot, core], near_norm.at[slot, core],
                norm_send.at[slot, core], norm_recv.at[slot, core], device(y, h, 1 - c, z, r),
            ).wait_recv()
            remote(
                near.at[slot, pl.ds(core * 128, 128)], near.at[slot, pl.ds(core * 128, 128)],
                gather_send.at[slot, core], gather_recv.at[slot, core], device(y, h, 1 - c, z, r),
            ).wait_recv()

    arrived(OUT)
    far_copy = remote(near.at[OUT], near.at[FAR], far_sem.at[0], far_sem.at[1], device(y + 2, h, c, z, r))
    far_norm = remote(near_norm.at[OUT], near_norm.at[FAR], far_sem.at[2], far_sem.at[3], device(y + 2, h, c, z, r))

    @pl.when(even_chip)
    def _():
        far_copy.start()
        far_norm.start()

    arrived(UP)
    arrived(DOWN)
    for tile in tiles_of(1):
        product(tile)
    for kind in (UP, DOWN):
        spread_norms(kind)
    start_pairs(1)
    finish_batch(0)
    start_codes(1)

    @pl.when(even_chip)
    def _():
        far_copy.wait_recv()
        far_norm.wait_recv()

    for tile in tiles_of(2):
        product(tile)
    start_pairs(2)
    finish_batch(1)
    start_codes(2)
    finish_batch(2)

    pltpu.make_async_copy(staging, staging, final_recv).wait()
    for half in range(2):
        direct = is_direct(dp, z, r, half)

        @pl.when(direct)
        def _():
            out_ref[pl.ds(half * 128, 128), :] = staging[half]

        @pl.when(jnp.logical_not(direct))
        def _():
            out_ref[pl.ds(half * 128, 128), :] = staging[half].T

    waits = sends + square_sends + own_sends + norm_sends + core_sends
    for batch in range(3):
        waits += pairs[batch] + code_sends[batch]
    for copy in waits:
        copy.wait_send()

    @pl.when(even_chip)
    def _():
        far_copy.wait_send()
        far_norm.wait_send()

    for copy, here in final_waits:

        @pl.when(jnp.logical_not(here))
        def _():
            copy.wait_send()


def body(grads):
    dma = pltpu.SemaphoreType.DMA
    return pl.pallas_call(
        kernel,
        out_shape=jax.ShapeDtypeStruct((256, 128), F32),
        in_specs=[pl.BlockSpec(memory_space=pltpu.VMEM)],
        out_specs=pl.BlockSpec(memory_space=pltpu.VMEM),
        scratch_shapes=[
            pltpu.VMEM((4, 256, HALF), BF16),
            pltpu.VMEM((2, 256, HALF), BF16),
            pltpu.VMEM((TILE_COUNT, 2, 256, 128), F32),
            pltpu.VMEM((TILE_COUNT, 256, 128), F32),
            pltpu.VMEM((TILE_COUNT, 4, 64, 128), F32),
            pltpu.VMEM((2, TILE_COUNT, 64, 128), F32),
            pltpu.VMEM((8, TILE_COUNT, 16, 128), BF16),
            pltpu.VMEM((8, TILE_COUNT, 16, 128), BF16),
            pltpu.VMEM((TILE_COUNT, 16, 128), F32),
            pltpu.VMEM((2, 128, 128), F32),
            pltpu.VMEM((16, 1, 256), F32),
            pltpu.VMEM((2, 1, 128), F32),
            pltpu.VMEM((4, 2, 1, 128), F32),
            pltpu.VMEM((2, 2, 1, 128), F32),
            pltpu.VMEM((5, 4, 64, 128), F32),
            dma((3, 2)),
            dma((3, 2)),
            dma((2,)),
            dma((2,)),
            dma((2,)),
            dma((4,)),
            dma((16,)),
            dma((16,)),
            dma((5, 2)),
            dma((5, 2)),
            dma((TILE_COUNT,)),
            dma((TILE_COUNT,)),
            dma((3, 2)),
            dma((3, 2)),
            dma((3, 8)),
            dma((3, 8)),
            dma((TILE_COUNT, 2)),
            dma,
        ],
        compiler_params=pltpu.CompilerParams(
            collective_id=0, has_side_effects=True, vmem_limit_bytes=40 * 1024 * 1024
        ),
        cost_estimate=pl.CostEstimate(flops=1510000000, bytes_accessed=1500000, transcendentals=0),
    )(grads)


def solution(mesh):
    in_specs = (P("dp", "layer"),)
    out_specs = P("dp", ("layer", "rep"))
    return jax.shard_map(body, mesh=mesh, in_specs=in_specs, out_specs=out_specs, check_vma=False)
```

```python
import functools

import jax
import jax.numpy as jnp
from jax import lax
from jax.experimental import pallas as pl
from jax.experimental.pallas import tpu as pltpu
from jax.sharding import PartitionSpec as P

MESH = pl.DeviceIdType.MESH
F32 = jnp.float32
BF16 = jnp.bfloat16
FEATURES = 2560
HALF = FEATURES // 2
CODE_SHIFT = 2.0**-7.5
CODE_SCALE = 13.4
UP, DOWN, OUT, FAR, OWN0, OWN1 = range(6)
TILE_COUNT = 9
BATCHES = ((0, 2), (2, 2), (4, 3), (7, 2))


def edge_bit(h, y):
    return (h + (3 - y % 4) // 3) % 2


def is_direct(dp, layer, rep, half):
    yd, hd = dp // 4, (dp // 2) % 2
    yl, hl = layer // 4, (layer // 2) % 2
    dh, dy = (hl + hd) % 2, (yl - yd + 4) % 4
    parity = (hd + yd) % 2
    mixed = (half + rep) % 2
    above = edge_bit(hd, yd)
    second = edge_bit(hd, yd + 1)
    below = edge_bit(hd, yd + 3)
    same_column = jnp.where(
        dy == 0,
        jnp.where(mixed == 0, 0, half),
        jnp.where(
            dy == 1,
            (mixed + parity + above) % 2,
            jnp.where(dy == 3, (mixed + parity + below) % 2, (mixed + above + second + 1) % 2),
        ),
    )
    other_column = jnp.where(
        dy == 1,
        (mixed + above) % 2,
        jnp.where(dy == 3, (mixed + below) % 2, jnp.where(dy == 0, 1 - parity, parity)),
    )
    return jnp.where(dh == 0, same_column, other_column) == 0


def encode(value):
    power = jnp.abs(value) * CODE_SCALE + CODE_SHIFT * CODE_SCALE
    for _ in range(5):
        power = power * power
    return jnp.where(value == 0.0, 0.0, jnp.where(value < 0.0, -power, power)).astype(BF16)


def decode(code):
    wide = code.astype(F32)
    size = jnp.abs(wide)
    root = jnp.maximum(size, 1e-37)
    for _ in range(4):
        root = lax.rsqrt(root)
    value = root * lax.rsqrt(root) * (1.0 / CODE_SCALE) - CODE_SHIFT
    return jnp.where(size < 1e-37, 0.0, jnp.where(wide < 0.0, -value, value))


def kernel(
    grads_ref, out_ref, g_ref, near, part, other, total, pair_code, paired, code, codes, final, staging,
    squares, norm, near_norm, row_scale,
    gather_send, gather_recv, own_send, own_recv, local_sem, far_sem, square_send, square_recv,
    norm_send, norm_recv, core_send, core_recv, pair_send, pair_recv, code_send, code_recv,
    final_send, final_recv, load_sem,
):
    dp = lax.axis_index("dp")
    z = lax.axis_index("layer")
    r = lax.axis_index("rep")
    y, h, c = dp // 4, (dp // 2) % 2, dp % 2
    parity = (h + y) % 2
    g = (r + parity) % 2
    odd = z % 2
    even_chip = parity == 0
    last_slot = OUT + 1 - parity

    def device(y_, h_, c_, z_, r_):
        return (4 * ((y_ + 4) % 4) + 2 * (h_ % 2) + c_, (z_ + 16) % 16, r_)

    def remote(src, dst, send, recv, target):
        return pltpu.make_async_remote_copy(
            src_ref=src, dst_ref=dst, send_sem=send, recv_sem=recv, device_id=target, device_id_type=MESH
        )

    load = pltpu.make_async_copy(grads_ref, g_ref, load_sem)
    load.start()

    barrier = pltpu.get_barrier_semaphore()
    partners = [device(y, h, 1 - c, z, r), device(y, h, c, z, 1 - r), device(y + 2, h, c, z, r)]
    partners += [device(y + 1, h + 1, c, z, 1 - r), device(y + 3, h + 1, c, z, 1 - r)]
    for core in range(2):
        partners += [device(y + 1, h, core, z, r), device(y + 3, h, core, z, r), device(y, h + 1, core, z, 1 - r)]
    for target in partners:
        pl.semaphore_signal(barrier, inc=1, device_id=target, device_id_type=MESH)
    for step in range(1, 16):
        pl.semaphore_signal(barrier, inc=1, device_id=device(y, h, c, z + step, r), device_id_type=MESH)

    load.wait()

    @pl.loop(0, 8)
    def _(group):
        wide = g_ref[pl.ds(pl.multiple_of(group * 32, 32), 32), :].astype(F32)
        local = jnp.sum(wide * wide, axis=1, keepdims=True)
        row_scale[0, pl.ds(pl.multiple_of(group * 32, 32), 32)] = jnp.broadcast_to(local, (32, 128))

    squares[z] = row_scale[0].T[0:1, :]

    pl.semaphore_wait(barrier, len(partners) + 15)

    wants = (
        (UP, (r + edge_bit(h, y + 3)) % 2, y + 3, h, r),
        (DOWN, (r + edge_bit(h, y)) % 2, y + 1, h, r),
        (OUT, 1 - r, y, h + 1, 1 - r),
    )
    def gather_copies(slot, half, y_, h_, r_):
        rows = pl.ds(pl.multiple_of(half * 128, 128), 128)
        return [
            remote(
                g_ref.at[rows, pl.ds(core * HALF, HALF)],
                near.at[slot, pl.ds(pl.multiple_of(c * 128, 128), 128)],
                gather_send.at[slot, core],
                gather_recv.at[slot, c],
                device(y_, h_, core, z, r_),
            )
            for core in range(2)
        ]

    gather = [copy for want in wants for copy in gather_copies(*want)]
    for copy in gather:
        copy.start()
    square_sends = []
    for step in range(1, 16):
        square_sends.append(
            remote(
                squares.at[z], squares.at[z], square_send.at[step], square_recv.at[z],
                device(y, h, c, z + step, r),
            )
        )
        square_sends[-1].start()
    mine = pl.ds(pl.multiple_of(c * HALF, 128), HALF)
    theirs = pl.ds(pl.multiple_of((1 - c) * HALF, 128), HALF)
    place = pl.ds(pl.multiple_of(c * 128, 128), 128)
    own_sends = []
    own_copies = []
    for half in range(2):
        rows = pl.ds(half * 128, 128)
        own_sends.append(
            remote(
                g_ref.at[rows, theirs], near.at[OWN0 + half, place], own_send.at[half], own_recv.at[half],
                device(y, h, 1 - c, z, r),
            )
        )
        own_copies.append(pltpu.make_async_copy(g_ref.at[rows, mine], near.at[OWN0 + half, place], local_sem.at[half]))
    for copy in own_sends + own_copies:
        copy.start()

    def choose(tile, values):
        chosen = values[-1]
        for index in range(len(values) - 2, -1, -1):
            chosen = jnp.where(tile == index, values[index], chosen)
        return chosen

    own = OWN0 + g

    def slots(tile):
        left = choose(tile, (own, OWN0, own, own, UP, UP, DOWN, OWN0, OWN1))
        right = choose(tile, (own, OWN1, UP, DOWN, DOWN, OUT, OUT, last_slot, last_slot))
        return left, right

    def core_copy(tile):
        return remote(
            part.at[tile, 1 - c], other.at[tile], core_send.at[tile], core_recv.at[tile], device(y, h, 1 - c, z, r)
        )

    def over_tiles(batch, step):
        first, count = BATCHES[batch]
        pl.loop(first, first + count)(step)

    def product(tile):
        left, right = slots(tile)
        value = lax.dot_general(near[left], near[right], (((1,), (1,)), ((), ())), preferred_element_type=F32)
        part[tile, 0] = value[:, 0:128]
        part[tile, 1] = value[:, 128:256]
        core_copy(tile).start()

    pair_targets = (device(y, h, c, z + 1 - 2 * odd, r), device(y, h, c, z - 1 + 2 * odd, r))

    def pair_copy(side, tile):
        return remote(
            pair_code.at[side, tile], paired.at[side, tile], pair_send.at[tile, side], pair_recv.at[tile, side],
            pair_targets[side],
        )

    def join_cores(tile):
        left, right = slots(tile)
        core_copy(tile).wait_recv()
        value = (part[tile, c] + other[tile]) * row_scale[left] * near_norm[right, c]
        total[tile] = value.reshape(4, 64, 128)
        for side in range(2):
            pair_code[side, tile] = encode(total[tile, 2 * side + 1 - odd])
            pair_copy(side, tile).start()

    def spread_norms(slot):
        for half in range(2):
            row_scale[slot, pl.ds(128 * half, 128)] = jnp.broadcast_to(near_norm[slot, half], (128, 128)).T

    def encode_tile(tile):
        for side in range(2):
            pair_copy(side, tile).wait_recv()
            coded = encode(total[tile, 2 * side + odd] + decode(paired[side, tile]))
            for j in range(4):
                code[2 * j + side, tile] = coded[16 * j : 16 * j + 16]

    def code_copies(batch):
        first, count = BATCHES[batch]
        copies = []
        for step in range(1, 8):
            slot = (z // 2 + step) % 8
            copies.append(
                remote(
                    code.at[slot, pl.ds(first, count)], codes.at[z // 2, pl.ds(first, count)],
                    code_send.at[batch, step], code_recv.at[batch, z // 2],
                    device(y, h, c, 2 * slot + odd, r),
                )
            )
        return copies

    def wait_codes(batch):
        first, count = BATCHES[batch]
        for step in range(1, 8):
            slot = (z // 2 + step) % 8
            remote(
                codes.at[slot, pl.ds(first, count)], codes.at[slot, pl.ds(first, count)],
                code_send.at[batch, step], code_recv.at[batch, slot],
                device(y, h, c, 2 * slot + odd, r),
            ).wait_recv()

    def sum_codes(tile):
        def add(step, value):
            return value + decode(codes[(z // 2 + step) % 8, tile])

        final[tile] = encode(lax.fori_loop(1, 8, add, decode(code[z // 2, tile])))

    row_block = (z % 4) // 2
    offset = pl.multiple_of(64 * (z % 2) + 16 * (z // 4), 16)
    strip = pl.ds(offset, 16)
    def places(slot):
        y_ = choose(slot, (y + 1, y + 3, y, y + 2, y, y))
        h_ = choose(slot, (h, h, h + 1, h + 1, h, h))
        far_set = jnp.where(c == 1, (1 - r + edge_bit(h + 1, y + 1)) % 2, r)
        set_ = choose(slot, ((r + edge_bit(h, y)) % 2, (r + edge_bit(h, y + 3)) % 2, r, far_set, 0, 1))
        return 4 * (y_ % 4) + 2 * (h_ % 2), set_

    def deliver(tile, number, wait=False):
        left, right = slots(tile)
        row, left_set = places(left)
        column, right_set = places(right)
        row, column = row + row_block, column + c
        mirror = number == 1
        dp_ = jnp.where(mirror, column, row)
        z_ = jnp.where(mirror, row, column)
        r_ = jnp.where(mirror, left_set, right_set)
        half = jnp.where(mirror, right_set, left_set)
        copy = remote(final.at[tile], staging.at[half, strip], final_send.at[tile, number], final_recv, (dp_, z_, r_))
        here = jnp.logical_and(jnp.logical_and(dp_ == dp, z_ == z), r_ == r)
        stay = pltpu.make_async_copy(final.at[tile], staging.at[half, strip], final_recv)

        @pl.when(jnp.logical_not(here))
        def _():
            if wait:
                copy.wait_send()
            else:
                copy.start()

        if not wait:

            @pl.when(here)
            def _():
                stay.start()

    def deliver_tile(tile, wait=False):
        @pl.loop(0, jnp.where(tile < 2, 1, 2))
        def _(number):
            deliver(tile, jnp.where(tile == 1, r, number), wait)

    def finish_tile(tile):
        sum_codes(tile)
        deliver_tile(tile)

    def finish_batch(batch):
        wait_codes(batch)
        over_tiles(batch, finish_tile)

    code_sends = [code_copies(batch) for batch in range(4)]

    def start_codes(batch):
        over_tiles(batch, encode_tile)
        for copy in code_sends[batch]:
            copy.start()

    for half in range(2):
        own_copies[half].wait()
        own_sends[half].wait_recv()
    over_tiles(0, product)

    for step in range(1, 16):
        source = (z + step) % 16
        remote(
            squares.at[source], squares.at[source], square_send.at[step], square_recv.at[source],
            device(y, h, c, z + step, r),
        ).wait_recv()
    inverse = lax.rsqrt(jnp.sum(squares[...], axis=0) + 1e-06)
    norm[0] = inverse[:, 0:128]
    norm[1] = inverse[:, 128:256]
    norm_sends = []
    for slot, half, y_, h_, r_ in wants:
        for core in range(2):
            norm_sends.append(
                remote(
                    norm.at[half], near_norm.at[slot, c], norm_send.at[slot, core], norm_recv.at[slot, c],
                    device(y_, h_, core, z, r_),
                )
            )
    for half in range(2):
        near_norm[OWN0 + half, c] = norm[half]
        norm_sends.append(
            remote(
                norm.at[half], near_norm.at[OWN0 + half, c], norm_send.at[4, half], norm_recv.at[4, half],
                device(y, h, 1 - c, z, r),
            )
        )
    for copy in norm_sends:
        copy.start()

    for half in range(2):
        remote(
            near_norm.at[OWN0 + half, 1 - c], near_norm.at[OWN0 + half, 1 - c], norm_send.at[4, half], norm_recv.at[4, half],
            device(y, h, 1 - c, z, r),
        ).wait_recv()
    for slot in (OWN0, OWN1):
        spread_norms(slot)
    over_tiles(0, join_cores)

    start_codes(0)

    def norm_arrived(slot):
        for core in range(2):
            remote(
                near_norm.at[slot, core], near_norm.at[slot, core],
                norm_send.at[slot, core], norm_recv.at[slot, core], device(y, h, 1 - c, z, r),
            ).wait_recv()

    def arrived(slot):
        for core in range(2):
            remote(
                near.at[slot, pl.ds(core * 128, 128)], near.at[slot, pl.ds(core * 128, 128)],
                gather_send.at[slot, core], gather_recv.at[slot, core], device(y, h, 1 - c, z, r),
            ).wait_recv()

    for slot in (UP, DOWN, OUT):
        norm_arrived(slot)
    for slot in (UP, DOWN):
        spread_norms(slot)

    for slot in (OUT, UP, DOWN):
        arrived(slot)
    far_copies = []
    for number, (slot, target) in enumerate(
        ((OUT, device(y + 2, h, c, z, r)), (UP, device(y + 3, h + 1, c, z, 1 - r)))
    ):
        rows = pl.ds(128 * number, 128)
        far_copies.append(
            remote(near.at[slot, rows], near.at[FAR, rows], far_sem.at[0, number], far_sem.at[1, number], target)
        )
        far_copies.append(
            remote(
                near_norm.at[slot, number], near_norm.at[FAR, number],
                far_sem.at[2, number], far_sem.at[3, number], target,
            )
        )

    @pl.when(even_chip)
    def _():
        for copy in far_copies:
            copy.start()

    over_tiles(1, product)
    over_tiles(2, product)
    over_tiles(1, join_cores)
    over_tiles(2, join_cores)
    start_codes(1)
    start_codes(2)
    finish_batch(0)

    @pl.when(even_chip)
    def _():
        for copy in far_copies:
            copy.wait_recv()

    over_tiles(3, product)
    over_tiles(3, join_cores)
    start_codes(3)
    finish_batch(1)
    finish_batch(2)
    finish_batch(3)

    pltpu.make_async_copy(staging, staging, final_recv).wait()
    for half in range(2):
        direct = is_direct(dp, z, r, half)

        @pl.when(direct)
        def _():
            out_ref[pl.ds(half * 128, 128), :] = decode(staging[half])

        @pl.when(jnp.logical_not(direct))
        def _():
            out_ref[pl.ds(half * 128, 128), :] = decode(staging[half]).T

    waits = gather + square_sends + own_sends + norm_sends
    for batch in range(4):
        waits += code_sends[batch]
    for copy in waits:
        copy.wait_send()

    @pl.when(even_chip)
    def _():
        for copy in far_copies:
            copy.wait_send()

    @pl.loop(0, TILE_COUNT)
    def _(tile):
        core_copy(tile).wait_send()
        for side in range(2):
            pair_copy(side, tile).wait_send()
        deliver_tile(tile, wait=True)


def body(grads):
    dma = pltpu.SemaphoreType.DMA
    return pl.pallas_call(
        kernel,
        out_shape=jax.ShapeDtypeStruct((256, 128), F32),
        in_specs=[pl.BlockSpec(memory_space=pltpu.HBM)],
        out_specs=pl.BlockSpec(memory_space=pltpu.VMEM),
        scratch_shapes=[
            pltpu.VMEM((256, FEATURES), BF16),
            pltpu.VMEM((6, 256, HALF), BF16),
            pltpu.VMEM((TILE_COUNT, 2, 256, 128), F32),
            pltpu.VMEM((TILE_COUNT, 256, 128), F32),
            pltpu.VMEM((TILE_COUNT, 4, 64, 128), F32),
            pltpu.VMEM((2, TILE_COUNT, 64, 128), BF16),
            pltpu.VMEM((2, TILE_COUNT, 64, 128), BF16),
            pltpu.VMEM((8, TILE_COUNT, 16, 128), BF16),
            pltpu.VMEM((8, TILE_COUNT, 16, 128), BF16),
            pltpu.VMEM((TILE_COUNT, 16, 128), BF16),
            pltpu.VMEM((2, 128, 128), BF16),
            pltpu.VMEM((16, 1, 256), F32),
            pltpu.VMEM((2, 1, 128), F32),
            pltpu.VMEM((6, 2, 1, 128), F32),
            pltpu.VMEM((6, 256, 128), F32),
            dma((3, 2)),
            dma((3, 2)),
            dma((2,)),
            dma((2,)),
            dma((2,)),
            dma((4, 2)),
            dma((16,)),
            dma((16,)),
            dma((5, 2)),
            dma((5, 2)),
            dma((TILE_COUNT,)),
            dma((TILE_COUNT,)),
            dma((TILE_COUNT, 2)),
            dma((TILE_COUNT, 2)),
            dma((4, 8)),
            dma((4, 8)),
            dma((TILE_COUNT, 2)),
            dma,
            dma,
        ],
        compiler_params=pltpu.CompilerParams(
            collective_id=0, has_side_effects=True, vmem_limit_bytes=60 * 1024 * 1024
        ),
        cost_estimate=pl.CostEstimate(flops=1510000000, bytes_accessed=1500000, transcendentals=0),
    )(grads)


def solution(mesh):
    in_specs = (P("dp", "layer"),)
    out_specs = P("dp", ("layer", "rep"))
    return jax.shard_map(body, mesh=mesh, in_specs=in_specs, out_specs=out_specs, check_vma=False)
```

```python
import functools

import jax
import jax.numpy as jnp
from jax import lax
from jax.experimental import pallas as pl
from jax.experimental.pallas import tpu as pltpu
from jax.sharding import PartitionSpec as P

MESH = pl.DeviceIdType.MESH
F32 = jnp.float32
BF16 = jnp.bfloat16
FEATURES = 2560
HALF = FEATURES // 2
CODE_SHIFT = 2.0**-7.5
CODE_SCALE = 13.4
UP, DOWN, OUT, FAR, OWN0, OWN1 = range(6)
TILE_COUNT = 9
BATCHES = ((0, 2), (2, 2), (4, 3), (7, 2))


def edge_bit(h, y):
    return (h + (3 - y % 4) // 3) % 2


def is_direct(dp, layer, rep, half):
    yd, hd = dp // 4, (dp // 2) % 2
    yl, hl = layer // 4, (layer // 2) % 2
    dh, dy = (hl + hd) % 2, (yl - yd + 4) % 4
    parity = (hd + yd) % 2
    mixed = (half + rep) % 2
    above = edge_bit(hd, yd)
    second = edge_bit(hd, yd + 1)
    below = edge_bit(hd, yd + 3)
    same_column = jnp.where(
        dy == 0,
        jnp.where(mixed == 0, 0, half),
        jnp.where(
            dy == 1,
            (mixed + parity + above) % 2,
            jnp.where(dy == 3, (mixed + parity + below) % 2, (mixed + above + second + 1) % 2),
        ),
    )
    other_column = jnp.where(
        dy == 1,
        (mixed + above) % 2,
        jnp.where(dy == 3, (mixed + below) % 2, jnp.where(dy == 0, 1 - parity, parity)),
    )
    return jnp.where(dh == 0, same_column, other_column) == 0


def encode(value):
    power = jnp.abs(value) * CODE_SCALE + CODE_SHIFT * CODE_SCALE
    for _ in range(5):
        power = power * power
    return jnp.where(value == 0.0, 0.0, jnp.where(value < 0.0, -power, power)).astype(BF16)


def decode(code):
    wide = code.astype(F32)
    size = jnp.abs(wide)
    root = jnp.maximum(size, 1e-37)
    for _ in range(4):
        root = lax.rsqrt(root)
    value = root * lax.rsqrt(root) * (1.0 / CODE_SCALE) - CODE_SHIFT
    return jnp.where(size < 1e-37, 0.0, jnp.where(wide < 0.0, -value, value))


def kernel(
    grads_ref, out_ref, g_ref, near, part, other, total, pair_code, paired, code, codes, final, staging,
    squares, norm, near_norm, row_scale,
    gather_send, gather_recv, own_send, own_recv, local_sem, far_sem, square_send, square_recv,
    norm_send, norm_recv, core_send, core_recv, pair_send, pair_recv, code_send, code_recv,
    final_send, final_recv, load_sem,
):
    dp = lax.axis_index("dp")
    z = lax.axis_index("layer")
    r = lax.axis_index("rep")
    y, h, c = dp // 4, (dp // 2) % 2, dp % 2
    parity = (h + y) % 2
    g = (r + parity) % 2
    quarter = z % 4
    even_chip = parity == 0
    odd_chip = parity == 1
    last_slot = OUT + 1 - parity

    def device(y_, h_, c_, z_, r_):
        return (4 * ((y_ + 4) % 4) + 2 * (h_ % 2) + c_, (z_ + 16) % 16, r_)

    def remote(src, dst, send, recv, target):
        return pltpu.make_async_remote_copy(
            src_ref=src, dst_ref=dst, send_sem=send, recv_sem=recv, device_id=target, device_id_type=MESH
        )

    load = pltpu.make_async_copy(grads_ref, g_ref, load_sem)
    load.start()

    barrier = pltpu.get_barrier_semaphore()
    partners = [device(y, h, 1 - c, z, r), device(y, h, c, z, 1 - r), device(y + 2, h, c, z, r)]
    partners += [device(y + 1, h + 1, c, z, 1 - r), device(y + 3, h + 1, c, z, 1 - r)]
    for core in range(2):
        partners += [device(y + 1, h, core, z, r), device(y + 3, h, core, z, r), device(y, h + 1, core, z, 1 - r)]
    for target in partners:
        pl.semaphore_signal(barrier, inc=1, device_id=target, device_id_type=MESH)
    for step in range(1, 16):
        pl.semaphore_signal(barrier, inc=1, device_id=device(y, h, c, z + step, r), device_id_type=MESH)

    load.wait()

    @pl.loop(0, 8)
    def _(group):
        wide = g_ref[pl.ds(pl.multiple_of(group * 32, 32), 32), :].astype(F32)
        local = jnp.sum(wide * wide, axis=1, keepdims=True)
        row_scale[0, pl.ds(pl.multiple_of(group * 32, 32), 32)] = jnp.broadcast_to(local, (32, 128))

    squares[z] = row_scale[0].T[0:1, :]

    pl.semaphore_wait(barrier, len(partners) + 15)

    wants = (
        (UP, (r + edge_bit(h, y + 3)) % 2, y + 3, h, r),
        (DOWN, (r + edge_bit(h, y)) % 2, y + 1, h, r),
        (OUT, 1 - r, y, h + 1, 1 - r),
    )
    def gather_copies(slot, half, y_, h_, r_):
        rows = pl.ds(pl.multiple_of(half * 128, 128), 128)
        return [
            remote(
                g_ref.at[rows, pl.ds(core * HALF, HALF)],
                near.at[slot, pl.ds(pl.multiple_of(c * 128, 128), 128)],
                gather_send.at[slot, core],
                gather_recv.at[slot, c],
                device(y_, h_, core, z, r_),
            )
            for core in range(2)
        ]

    gather = [copy for want in wants for copy in gather_copies(*want)]
    for copy in gather:
        copy.start()
    square_sends = []
    for step in range(1, 16):
        square_sends.append(
            remote(
                squares.at[z], squares.at[z], square_send.at[step], square_recv.at[z],
                device(y, h, c, z + step, r),
            )
        )
        square_sends[-1].start()
    mine = pl.ds(pl.multiple_of(c * HALF, 128), HALF)
    theirs = pl.ds(pl.multiple_of((1 - c) * HALF, 128), HALF)
    place = pl.ds(pl.multiple_of(c * 128, 128), 128)
    own_sends = []
    own_copies = []
    for half in range(2):
        rows = pl.ds(half * 128, 128)
        own_sends.append(
            remote(
                g_ref.at[rows, theirs], near.at[OWN0 + half, place], own_send.at[half], own_recv.at[half],
                device(y, h, 1 - c, z, r),
            )
        )
        own_copies.append(pltpu.make_async_copy(g_ref.at[rows, mine], near.at[OWN0 + half, place], local_sem.at[half]))
    for copy in own_sends + own_copies:
        copy.start()

    def choose(tile, values):
        chosen = values[-1]
        for index in range(len(values) - 2, -1, -1):
            chosen = jnp.where(tile == index, values[index], chosen)
        return chosen

    own = OWN0 + g

    def slots(tile):
        left = choose(tile, (own, OWN0, own, own, UP, UP, DOWN, OWN0, OWN1))
        right = choose(tile, (own, OWN1, UP, DOWN, DOWN, OUT, OUT, last_slot, last_slot))
        return left, right

    def core_copy(tile):
        return remote(
            part.at[tile, 1 - c], other.at[tile], core_send.at[tile], core_recv.at[tile], device(y, h, 1 - c, z, r)
        )

    def over_tiles(batch, step):
        first, count = BATCHES[batch]
        pl.loop(first, first + count)(step)

    def product(tile):
        left, right = slots(tile)
        value = lax.dot_general(near[left], near[right], (((1,), (1,)), ((), ())), preferred_element_type=F32)
        part[tile, 0] = value[:, 0:128]
        part[tile, 1] = value[:, 128:256]
        core_copy(tile).start()

    lanes = (
        (device(y, h, c, z - 1, r), 0, 0, 64),
        (device(y, h, c, z + 1, r), 1, 0, 64),
        (device(y, h, c, z + 2, r), 2, 0, 32),
        (device(y, h, c, z - 2, r), 2, 32, 32),
    )

    def near_copy(lane, tile):
        target, place_, start, size = lanes[lane]
        rows = pl.ds(start, size)
        return remote(
            pair_code.at[place_, tile, rows], paired.at[place_, tile, rows],
            pair_send.at[tile, lane], pair_recv.at[tile, lane], target,
        )

    def join_cores(tile):
        left, right = slots(tile)
        core_copy(tile).wait_recv()
        value = (part[tile, c] + other[tile]) * row_scale[left] * near_norm[right, c]
        total[tile] = value.reshape(4, 64, 128)
        for index, step in enumerate((3, 1, 2)):
            pair_code[index, tile] = encode(total[tile, (quarter + step) % 4])
        for lane in range(4):
            near_copy(lane, tile).start()

    def spread_norms(slot):
        for half in range(2):
            row_scale[slot, pl.ds(128 * half, 128)] = jnp.broadcast_to(near_norm[slot, half], (128, 128)).T

    def encode_tile(tile):
        for lane in range(4):
            near_copy(lane, tile).wait_recv()
        value = total[tile, quarter] + jnp.sum(decode(paired[:, tile]), axis=0)
        coded = encode(value)
        for j in range(4):
            code[j, tile] = coded[16 * j : 16 * j + 16]
        codes[z // 4, tile] = code[z // 4, tile]

    def code_copies(batch):
        first, count = BATCHES[batch]
        copies = []
        for step in range(1, 4):
            slot = (z // 4 + step) % 4
            copies.append(
                remote(
                    code.at[slot, pl.ds(first, count)], codes.at[z // 4, pl.ds(first, count)],
                    code_send.at[batch, step], code_recv.at[batch, z // 4],
                    device(y, h, c, 4 * slot + quarter, r),
                )
            )
        return copies

    def wait_codes(batch):
        first, count = BATCHES[batch]
        for step in range(1, 4):
            slot = (z // 4 + step) % 4
            remote(
                codes.at[slot, pl.ds(first, count)], codes.at[slot, pl.ds(first, count)],
                code_send.at[batch, step], code_recv.at[batch, slot],
                device(y, h, c, 4 * slot + quarter, r),
            ).wait_recv()

    def sum_codes(tile):
        final[tile] = encode(jnp.sum(decode(codes[:, tile]), axis=0))

    row_block = (z % 4) // 2
    offset = pl.multiple_of(64 * (z % 2) + 16 * (z // 4), 16)
    strip = pl.ds(offset, 16)
    far_set = jnp.where(c == 1, (1 - r + edge_bit(h + 1, y + 1 + h)) % 2, r)
    home = 4 * y + 2 * h
    across = 2 - 2 * h
    places = {
        UP: (4 * ((y + 1) % 4) + 2 * h, (r + edge_bit(h, y)) % 2),
        DOWN: (4 * ((y + 3) % 4) + 2 * h, (r + edge_bit(h, y + 3)) % 2),
        OUT: (4 * y + across, r),
        OWN0: (home, 0),
        OWN1: (home, 1),
        "own": (home, g),
        "last": (4 * ((y + 2 - 2 * parity) % 4) + across, jnp.where(even_chip, far_set, r)),
    }
    pairs = (
        ("own", "own"), (OWN0, OWN1), ("own", UP), ("own", DOWN), (UP, DOWN), (UP, OUT), (DOWN, OUT),
        (OWN0, "last"), (OWN1, "last"),
    )
    strips = []
    for tile, (left, right) in enumerate(pairs):
        row, left_set = places[left]
        column, right_set = places[right]
        row, column = row + row_block, column + c
        owner = (row, column, right_set, left_set)
        mirror = (column, row, left_set, right_set)
        if tile == 0:
            targets = (owner,)
        elif tile == 1:
            targets = (tuple(jnp.where(r == 0, a, b) for a, b in zip(owner, mirror)),)
        else:
            targets = (owner, mirror)
        for number, (dp_, z_, r_, half) in enumerate(targets):
            copy = remote(
                final.at[tile], staging.at[half, strip], final_send.at[tile, number], final_recv, (dp_, z_, r_)
            )
            here = None
            if tile < 2 or (number == 0 and left in ("own", OWN0, OWN1)):
                here = jnp.logical_and(jnp.logical_and(dp_ == dp, z_ == z), r_ == r)
            strips.append((tile, copy, here, half))

    def deliver(tile):
        for tile_, copy, here, half in strips:
            if tile_ != tile:
                continue
            if here is None:
                copy.start()
            else:
                pl.when(jnp.logical_not(here))(copy.start)
                pl.when(here)(pltpu.make_async_copy(final.at[tile], staging.at[half, strip], final_recv).start)

    def finish_batch(batch):
        wait_codes(batch)
        first, count = BATCHES[batch]
        for tile in range(first, first + count):
            sum_codes(tile)
            deliver(tile)

    code_sends = [code_copies(batch) for batch in range(4)]

    def start_codes(batch):
        over_tiles(batch, encode_tile)
        for copy in code_sends[batch]:
            copy.start()

    for half in range(2):
        own_copies[half].wait()
        own_sends[half].wait_recv()
    over_tiles(0, product)

    for step in range(1, 16):
        source = (z + step) % 16
        remote(
            squares.at[source], squares.at[source], square_send.at[step], square_recv.at[source],
            device(y, h, c, z + step, r),
        ).wait_recv()
    inverse = lax.rsqrt(jnp.sum(squares[...], axis=0) + 1e-06)
    norm[0] = inverse[:, 0:128]
    norm[1] = inverse[:, 128:256]
    norm_sends = []
    for slot, half, y_, h_, r_ in wants:
        for core in range(2):
            norm_sends.append(
                remote(
                    norm.at[half], near_norm.at[slot, c], norm_send.at[slot, core], norm_recv.at[slot, c],
                    device(y_, h_, core, z, r_),
                )
            )
    for half in range(2):
        near_norm[OWN0 + half, c] = norm[half]
        norm_sends.append(
            remote(
                norm.at[half], near_norm.at[OWN0 + half, c], norm_send.at[4, half], norm_recv.at[4, half],
                device(y, h, 1 - c, z, r),
            )
        )
    for copy in norm_sends:
        copy.start()

    for half in range(2):
        remote(
            near_norm.at[OWN0 + half, 1 - c], near_norm.at[OWN0 + half, 1 - c], norm_send.at[4, half], norm_recv.at[4, half],
            device(y, h, 1 - c, z, r),
        ).wait_recv()
    for slot in (OWN0, OWN1):
        spread_norms(slot)
    over_tiles(0, join_cores)

    start_codes(0)

    def norm_arrived(slot):
        for core in range(2):
            remote(
                near_norm.at[slot, core], near_norm.at[slot, core],
                norm_send.at[slot, core], norm_recv.at[slot, core], device(y, h, 1 - c, z, r),
            ).wait_recv()

    def arrived(slot):
        for core in range(2):
            remote(
                near.at[slot, pl.ds(core * 128, 128)], near.at[slot, pl.ds(core * 128, 128)],
                gather_send.at[slot, core], gather_recv.at[slot, core], device(y, h, 1 - c, z, r),
            ).wait_recv()

    for slot in (UP, DOWN, OUT):
        norm_arrived(slot)
    for slot in (UP, DOWN):
        spread_norms(slot)

    for slot in (OUT, UP, DOWN):
        arrived(slot)
    far_copies = []
    for number, (slot, target) in enumerate(
        ((OUT, device(y + 2, h, c, z, r)), (DOWN - h, device(y + 1 + 2 * h, h + 1, c, z, 1 - r)))
    ):
        rows = pl.ds(128 * number, 128)
        far_copies.append(
            remote(near.at[slot, rows], near.at[FAR, rows], far_sem.at[0, number], far_sem.at[1, number], target)
        )
        far_copies.append(
            remote(
                near_norm.at[slot, number], near_norm.at[FAR, number],
                far_sem.at[2, number], far_sem.at[3, number], target,
            )
        )

    @pl.when(even_chip)
    def _():
        for copy in far_copies:
            copy.start()

    over_tiles(1, product)
    over_tiles(2, product)

    @pl.when(odd_chip)
    def _():
        over_tiles(3, product)

    over_tiles(1, join_cores)
    over_tiles(2, join_cores)

    @pl.when(odd_chip)
    def _():
        over_tiles(3, join_cores)

    start_codes(1)
    start_codes(2)

    @pl.when(odd_chip)
    def _():
        start_codes(3)

    finish_batch(0)

    @pl.when(even_chip)
    def _():
        for copy in far_copies:
            copy.wait_recv()
        over_tiles(3, product)
        over_tiles(3, join_cores)
        start_codes(3)

    finish_batch(1)
    finish_batch(2)
    finish_batch(3)

    waits = gather + square_sends + own_sends + norm_sends
    for batch in range(4):
        waits += code_sends[batch]
    for copy in waits:
        copy.wait_send()

    @pl.when(even_chip)
    def _():
        for copy in far_copies:
            copy.wait_send()

    @pl.loop(0, TILE_COUNT)
    def _(tile):
        core_copy(tile).wait_send()
        for lane in range(4):
            near_copy(lane, tile).wait_send()

    for _, copy, here, _ in strips:
        if here is None:
            copy.wait_send()
        else:
            pl.when(jnp.logical_not(here))(copy.wait_send)

    pltpu.make_async_copy(staging, staging, final_recv).wait()
    for half in range(2):
        direct = is_direct(dp, z, r, half)

        @pl.when(direct)
        def _():
            out_ref[pl.ds(half * 128, 128), :] = decode(staging[half])

        @pl.when(jnp.logical_not(direct))
        def _():
            out_ref[pl.ds(half * 128, 128), :] = decode(staging[half]).T


def body(grads):
    dma = pltpu.SemaphoreType.DMA
    return pl.pallas_call(
        kernel,
        out_shape=jax.ShapeDtypeStruct((256, 128), F32),
        in_specs=[pl.BlockSpec(memory_space=pltpu.HBM)],
        out_specs=pl.BlockSpec(memory_space=pltpu.VMEM),
        scratch_shapes=[
            pltpu.VMEM((256, FEATURES), BF16),
            pltpu.VMEM((6, 256, HALF), BF16),
            pltpu.VMEM((TILE_COUNT, 2, 256, 128), F32),
            pltpu.VMEM((TILE_COUNT, 256, 128), F32),
            pltpu.VMEM((TILE_COUNT, 4, 64, 128), F32),
            pltpu.VMEM((3, TILE_COUNT, 64, 128), BF16),
            pltpu.VMEM((3, TILE_COUNT, 64, 128), BF16),
            pltpu.VMEM((4, TILE_COUNT, 16, 128), BF16),
            pltpu.VMEM((4, TILE_COUNT, 16, 128), BF16),
            pltpu.VMEM((TILE_COUNT, 16, 128), BF16),
            pltpu.VMEM((2, 128, 128), BF16),
            pltpu.VMEM((16, 1, 256), F32),
            pltpu.VMEM((2, 1, 128), F32),
            pltpu.VMEM((6, 2, 1, 128), F32),
            pltpu.VMEM((6, 256, 128), F32),
            dma((3, 2)),
            dma((3, 2)),
            dma((2,)),
            dma((2,)),
            dma((2,)),
            dma((4, 2)),
            dma((16,)),
            dma((16,)),
            dma((5, 2)),
            dma((5, 2)),
            dma((TILE_COUNT,)),
            dma((TILE_COUNT,)),
            dma((TILE_COUNT, 4)),
            dma((TILE_COUNT, 4)),
            dma((4, 4)),
            dma((4, 4)),
            dma((TILE_COUNT, 2)),
            dma,
            dma,
        ],
        compiler_params=pltpu.CompilerParams(
            collective_id=0, has_side_effects=True, vmem_limit_bytes=60 * 1024 * 1024
        ),
        cost_estimate=pl.CostEstimate(flops=1510000000, bytes_accessed=1500000, transcendentals=0),
    )(grads)


def solution(mesh):
    in_specs = (P("dp", "layer"),)
    out_specs = P("dp", ("layer", "rep"))
    return jax.shard_map(body, mesh=mesh, in_specs=in_specs, out_specs=out_specs, check_vma=False)
```

```python
import functools

import jax
import jax.numpy as jnp
from jax import lax
from jax.experimental import pallas as pl
from jax.experimental.pallas import tpu as pltpu
from jax.sharding import PartitionSpec as P

MESH = pl.DeviceIdType.MESH
F32 = jnp.float32
BF16 = jnp.bfloat16
FEATURES = 2560
HALF = FEATURES // 2
CODE_SHIFT = 2.0**-7.5
CODE_SCALE = 13.4
UP, DOWN, OUT, FAR, OWN0, OWN1 = range(6)
TILE_COUNT = 11
BATCHES = ((0, 2), (2, 4), (6, 3), (9, 2))


def edge_bit(h, y):
    return (h + (3 - y % 4) // 3) % 2


def is_direct(dp, layer, rep, half):
    yd, hd = dp // 4, (dp // 2) % 2
    yl, hl = layer // 4, (layer // 2) % 2
    dh, dy = (hl + hd) % 2, (yl - yd + 4) % 4
    parity = (hd + yd + 1) % 2
    mixed = (half + rep) % 2
    above = edge_bit(hd, yd)
    second = edge_bit(hd, yd + 1)
    below = edge_bit(hd, yd + 3)
    same_column = jnp.where(
        dy == 0,
        jnp.where(mixed == 0, 0, half),
        jnp.where(dy == 2, (mixed + above + second + 1) % 2, 1 - parity),
    )
    other_column = jnp.where(
        dy == 1,
        (mixed + above) % 2,
        jnp.where(dy == 3, (mixed + below) % 2, jnp.where(dy == 0, 1 - parity, parity)),
    )
    return jnp.where(dh == 0, same_column, other_column) == 0


def encode(value):
    power = jnp.abs(value) * CODE_SCALE + CODE_SHIFT * CODE_SCALE
    for _ in range(5):
        power = power * power
    return jnp.where(value == 0.0, 0.0, jnp.where(value < 0.0, -power, power)).astype(BF16)


def decode(code):
    wide = code.astype(F32)
    size = jnp.abs(wide)
    root = jnp.maximum(size, 1e-37)
    for _ in range(4):
        root = lax.rsqrt(root)
    value = root * lax.rsqrt(root) * (1.0 / CODE_SCALE) - CODE_SHIFT
    return jnp.where(size < 1e-37, 0.0, jnp.where(wide < 0.0, -value, value))


def kernel(
    grads_ref, out_ref, g_ref, near, part, other, total, pair_code, paired, code, codes, final, staging,
    squares, norm, near_norm, row_scale,
    gather_send, gather_recv, own_send, own_recv, local_sem, far_sem, square_send, square_recv,
    norm_send, norm_recv, core_send, core_recv, pair_send, pair_recv, code_send, code_recv,
    final_send, final_recv, load_sem, entered,
):
    dp = lax.axis_index("dp")
    z = lax.axis_index("layer")
    r = lax.axis_index("rep")
    y, h, c = dp // 4, (dp // 2) % 2, dp % 2
    parity = (h + y + 1) % 2
    g = (r + parity) % 2
    quarter = z % 4
    even_chip = parity == 0
    odd_chip = parity == 1
    last_slot = OUT + 1 - parity

    def device(y_, h_, c_, z_, r_):
        return (4 * ((y_ + 4) % 4) + 2 * (h_ % 2) + c_, (z_ + 16) % 16, r_)

    def remote(src, dst, send, recv, target):
        return pltpu.make_async_remote_copy(
            src_ref=src, dst_ref=dst, send_sem=send, recv_sem=recv, device_id=target, device_id_type=MESH
        )

    load = pltpu.make_async_copy(grads_ref, g_ref, load_sem)
    load.start()

    barrier = pltpu.get_barrier_semaphore()
    partners = [device(y, h, 1 - c, z, r), device(y, h, c, z, 1 - r), device(y + 2, h, c, z, r)]
    partners += [device(y + 1, h + 1, c, z, 1 - r), device(y + 3, h + 1, c, z, 1 - r)]
    for core in range(2):
        partners += [device(y + 1, h, core, z, r), device(y + 3, h, core, z, r), device(y, h + 1, core, z, 1 - r)]
    partners += [device(y, h, c, z + step, r) for step in (-3, -2, -1, 1, 2, 3)]
    for target in partners:
        pl.semaphore_signal(barrier, inc=1, device_id=target, device_id_type=MESH)
    load.wait()
    pl.semaphore_wait(barrier, len(partners))

    wants = (
        (UP, (r + edge_bit(h, y + 3)) % 2, y + 3, h, r),
        (DOWN, (r + edge_bit(h, y)) % 2, y + 1, h, r),
        (OUT, 1 - r, y, h + 1, 1 - r),
    )
    def gather_copies(part_, slot, half, y_, h_, r_):
        rows = pl.ds(pl.multiple_of(half * 128 + part_ * 64, 64), 64)
        return [
            remote(
                g_ref.at[rows, pl.ds(core * HALF, HALF)],
                near.at[slot, pl.ds(pl.multiple_of(c * 128 + part_ * 64, 64), 64)],
                gather_send.at[slot, core, part_],
                gather_recv.at[slot, c, part_],
                device(y_, h_, core, z, r_),
            )
            for core in range(2)
        ]

    gather = [copy for part_ in range(2) for want in wants for copy in gather_copies(part_, *want)]
    for copy in gather:
        copy.start()
    mine = pl.ds(pl.multiple_of(c * HALF, 128), HALF)
    theirs = pl.ds(pl.multiple_of((1 - c) * HALF, 128), HALF)
    place = pl.ds(pl.multiple_of(c * 128, 128), 128)
    own_sends = []
    own_copies = []
    for half in range(2):
        rows = pl.ds(half * 128, 128)
        own_sends.append(
            remote(
                g_ref.at[rows, theirs], near.at[OWN0 + half, place], own_send.at[half], own_recv.at[half],
                device(y, h, 1 - c, z, r),
            )
        )
        own_copies.append(pltpu.make_async_copy(g_ref.at[rows, mine], near.at[OWN0 + half, place], local_sem.at[half]))
    for copy in own_sends + own_copies:
        copy.start()

    @pl.loop(0, 8)
    def _(group):
        wide = g_ref[pl.ds(pl.multiple_of(group * 32, 32), 32), :].astype(F32)
        local = jnp.sum(wide * wide, axis=1, keepdims=True)
        row_scale[0, pl.ds(pl.multiple_of(group * 32, 32), 32)] = jnp.broadcast_to(local, (32, 128))

    squares[z] = row_scale[0].T[0:1, :]
    for stage in range(2):
        for step in (-3, 3):
            pl.semaphore_signal(
                entered.at[stage], inc=1, device_id=device(y, h, c, z + step, r), device_id_type=MESH
            )
        pl.semaphore_wait(entered.at[stage], 2)
    square_sends = []
    for step in range(1, 16):
        square_sends.append(
            remote(
                squares.at[z], squares.at[z], square_send.at[step], square_recv.at[z],
                device(y, h, c, z + step, r),
            )
        )
        square_sends[-1].start()
    def choose(tile, values):
        chosen = values[-1]
        for index in range(len(values) - 2, -1, -1):
            chosen = jnp.where(tile == index, values[index], chosen)
        return chosen

    own = OWN0 + g

    def slots(tile):
        left = choose(tile, (own, OWN0, OWN0, OWN1, OWN0, OWN1, UP, UP, DOWN, OWN0, OWN1))
        right = choose(tile, (own, OWN1, UP, UP, DOWN, DOWN, DOWN, OUT, OUT, last_slot, last_slot))
        return left, right

    def core_copy(tile):
        return remote(
            part.at[tile, 1 - c], other.at[tile], core_send.at[tile], core_recv.at[tile], device(y, h, 1 - c, z, r)
        )

    def over_tiles(batch, step):
        first, count = BATCHES[batch]
        pl.loop(first, first + count)(step)

    def product(tile):
        left, right = slots(tile)
        value = lax.dot_general(near[left], near[right], (((1,), (1,)), ((), ())), preferred_element_type=F32)
        part[tile, 0] = value[:, 0:128]
        part[tile, 1] = value[:, 128:256]
        core_copy(tile).start()

    lanes = (
        (device(y, h, c, z - 1, r), 0, 0, 64),
        (device(y, h, c, z + 1, r), 1, 0, 64),
        (device(y, h, c, z + 2, r), 2, 0, 32),
        (device(y, h, c, z - 2, r), 2, 32, 32),
    )

    def near_copy(lane, tile):
        target, place_, start, size = lanes[lane]
        rows = pl.ds(start, size)
        return remote(
            pair_code.at[place_, tile, rows], paired.at[place_, tile, rows],
            pair_send.at[tile, lane], pair_recv.at[tile, lane], target,
        )

    def join_cores(tile):
        left, right = slots(tile)
        core_copy(tile).wait_recv()
        value = (part[tile, c] + other[tile]) * row_scale[left] * near_norm[right, c]
        total[tile] = value.reshape(4, 64, 128)
        for index, step in enumerate((3, 1, 2)):
            pair_code[index, tile] = encode(total[tile, (quarter + step) % 4])
        for lane in range(4):
            near_copy(lane, tile).start()

    def spread_norms(slot):
        for half in range(2):
            row_scale[slot, pl.ds(128 * half, 128)] = jnp.broadcast_to(near_norm[slot, half], (128, 128)).T

    def encode_tile(tile):
        for lane in range(4):
            near_copy(lane, tile).wait_recv()
        value = total[tile, quarter] + jnp.sum(decode(paired[:, tile]), axis=0)
        coded = encode(value)
        for j in range(4):
            code[j, tile] = coded[16 * j : 16 * j + 16]
        codes[z // 4, tile] = code[z // 4, tile]

    def code_copies(batch):
        first, count = BATCHES[batch]
        copies = []
        for step in range(1, 4):
            slot = (z // 4 + step) % 4
            copies.append(
                remote(
                    code.at[slot, pl.ds(first, count)], codes.at[z // 4, pl.ds(first, count)],
                    code_send.at[batch, step], code_recv.at[batch, z // 4],
                    device(y, h, c, 4 * slot + quarter, r),
                )
            )
        return copies

    def wait_codes(batch):
        first, count = BATCHES[batch]
        for step in range(1, 4):
            slot = (z // 4 + step) % 4
            remote(
                codes.at[slot, pl.ds(first, count)], codes.at[slot, pl.ds(first, count)],
                code_send.at[batch, step], code_recv.at[batch, slot],
                device(y, h, c, 4 * slot + quarter, r),
            ).wait_recv()

    def sum_codes(tile):
        final[tile] = encode(jnp.sum(decode(codes[:, tile]), axis=0))

    row_block = (z % 4) // 2
    offset = pl.multiple_of(64 * (z % 2) + 16 * (z // 4), 16)
    strip = pl.ds(offset, 16)
    far_set = jnp.where(c == 1, (1 - r + edge_bit(h + 1, y + 1 + y % 2)) % 2, r)
    home = 4 * y + 2 * h
    across = 2 - 2 * h
    places = {
        UP: (4 * ((y + 1) % 4) + 2 * h, (r + edge_bit(h, y)) % 2),
        DOWN: (4 * ((y + 3) % 4) + 2 * h, (r + edge_bit(h, y + 3)) % 2),
        OUT: (4 * y + across, r),
        OWN0: (home, 0),
        OWN1: (home, 1),
        "own": (home, g),
        "last": (4 * ((y + 2 - 2 * parity) % 4) + across, jnp.where(even_chip, far_set, r)),
    }
    pairs = (
        ("own", "own"), (OWN0, OWN1), (OWN0, UP), (OWN1, UP), (OWN0, DOWN), (OWN1, DOWN),
        (UP, DOWN), (UP, OUT), (DOWN, OUT), (OWN0, "last"), (OWN1, "last"),
    )
    strips = []
    for tile, (left, right) in enumerate(pairs):
        row, left_set = places[left]
        column, right_set = places[right]
        row, column = row + row_block, column + c
        owner = (row, column, right_set, left_set)
        mirror = (column, row, left_set, right_set)
        if tile == 0:
            targets = (owner,)
        elif tile == 1:
            targets = (tuple(jnp.where(r == 0, a, b) for a, b in zip(owner, mirror)),)
        else:
            targets = (owner, mirror)
        for number, (dp_, z_, r_, half) in enumerate(targets):
            copy = remote(
                final.at[tile], staging.at[half, strip], final_send.at[tile, number], final_recv, (dp_, z_, r_)
            )
            here = None
            if tile < 2 or (number == 0 and left in ("own", OWN0, OWN1)):
                here = jnp.logical_and(jnp.logical_and(dp_ == dp, z_ == z), r_ == r)
            strips.append((tile, copy, here, half))

    def deliver(tile):
        for tile_, copy, here, half in strips:
            if tile_ != tile:
                continue
            if here is None:
                copy.start()
            else:
                pl.when(jnp.logical_not(here))(copy.start)
                pl.when(here)(pltpu.make_async_copy(final.at[tile], staging.at[half, strip], final_recv).start)

    def finish_batch(batch):
        wait_codes(batch)
        first, count = BATCHES[batch]
        for tile in range(first, first + count):
            sum_codes(tile)
            deliver(tile)

    code_sends = [code_copies(batch) for batch in range(4)]

    def start_codes(batch):
        over_tiles(batch, encode_tile)
        for copy in code_sends[batch]:
            copy.start()

    for half in range(2):
        own_copies[half].wait()
        own_sends[half].wait_recv()
    over_tiles(0, product)

    for step in range(1, 16):
        source = (z + step) % 16
        remote(
            squares.at[source], squares.at[source], square_send.at[step], square_recv.at[source],
            device(y, h, c, z + step, r),
        ).wait_recv()
    inverse = lax.rsqrt(jnp.sum(squares[...], axis=0) + 1e-06)
    norm[0] = inverse[:, 0:128]
    norm[1] = inverse[:, 128:256]
    norm_sends = []
    for slot, half, y_, h_, r_ in wants:
        for core in range(2):
            norm_sends.append(
                remote(
                    norm.at[half], near_norm.at[slot, c], norm_send.at[slot, core], norm_recv.at[slot, c],
                    device(y_, h_, core, z, r_),
                )
            )
    for half in range(2):
        near_norm[OWN0 + half, c] = norm[half]
        norm_sends.append(
            remote(
                norm.at[half], near_norm.at[OWN0 + half, c], norm_send.at[4, half], norm_recv.at[4, half],
                device(y, h, 1 - c, z, r),
            )
        )
    for copy in norm_sends:
        copy.start()

    for half in range(2):
        remote(
            near_norm.at[OWN0 + half, 1 - c], near_norm.at[OWN0 + half, 1 - c], norm_send.at[4, half], norm_recv.at[4, half],
            device(y, h, 1 - c, z, r),
        ).wait_recv()
    for slot in (OWN0, OWN1):
        spread_norms(slot)
    over_tiles(0, join_cores)

    def norm_arrived(slot):
        for core in range(2):
            remote(
                near_norm.at[slot, core], near_norm.at[slot, core],
                norm_send.at[slot, core], norm_recv.at[slot, core], device(y, h, 1 - c, z, r),
            ).wait_recv()

    def arrived(slot, core, part_):
        rows = pl.ds(core * 128 + part_ * 64, 64)
        remote(
            near.at[slot, rows], near.at[slot, rows],
            gather_send.at[slot, core, part_], gather_recv.at[slot, core, part_], device(y, h, 1 - c, z, r),
        ).wait_recv()

    for slot in (UP, DOWN, OUT):
        norm_arrived(slot)
    for slot in (UP, DOWN):
        spread_norms(slot)

    far_copies = []

    def forward(number, part_):
        slot, target = (
            (OUT, device(y + 2, h, c, z, r)), (DOWN - y % 2, device(y + 1 + 2 * (y % 2), h + 1, c, z, 1 - r))
        )[number]
        arrived(slot, number, part_)
        rows = pl.ds(128 * number + 64 * part_, 64)
        copies = [
            remote(
                near.at[slot, rows], near.at[FAR, rows],
                far_sem.at[0, number, part_], far_sem.at[1, number, part_], target,
            )
        ]
        if part_ == 0:
            copies.append(
                remote(
                    near_norm.at[slot, number], near_norm.at[FAR, number],
                    far_sem.at[2, number, 0], far_sem.at[2, number, 1], target,
                )
            )

        @pl.when(even_chip)
        def _():
            for copy in copies:
                copy.start()

        far_copies.extend(copies)

    forward(0, 0)
    forward(1, 0)
    start_codes(0)

    forward(0, 1)
    forward(1, 1)
    for part_ in range(2):
        arrived(OUT, 1, part_)
        arrived(DOWN - y % 2, 0, part_)
        for core in range(2):
            arrived(UP + y % 2, core, part_)

    @pl.when(odd_chip)
    def _():
        over_tiles(1, product)
        over_tiles(2, product)
        over_tiles(1, join_cores)
        over_tiles(3, product)
        over_tiles(2, join_cores)
        over_tiles(3, join_cores)
        start_codes(1)
        start_codes(2)
        start_codes(3)
        finish_batch(0)
        finish_batch(1)
        finish_batch(2)
        finish_batch(3)

    @pl.when(even_chip)
    def _():
        over_tiles(2, product)
        over_tiles(2, join_cores)
        start_codes(2)
        finish_batch(0)
        for copy in far_copies:
            copy.wait_recv()
        over_tiles(3, product)
        over_tiles(3, join_cores)
        finish_batch(2)
        start_codes(3)
        finish_batch(3)

    waits = gather + square_sends + own_sends + norm_sends
    for batch in (0, 2, 3):
        waits += code_sends[batch]
    for copy in waits:
        copy.wait_send()

    def sent(tile):
        core_copy(tile).wait_send()
        for lane in range(4):
            near_copy(lane, tile).wait_send()

    def delivered(batch):
        first, count = BATCHES[batch]
        for tile, copy, here, _ in strips:
            if not first <= tile < first + count:
                continue
            if here is None:
                copy.wait_send()
            else:
                pl.when(jnp.logical_not(here))(copy.wait_send)

    for batch in (0, 2, 3):
        over_tiles(batch, sent)

    @pl.when(odd_chip)
    def _():
        for copy in code_sends[1]:
            copy.wait_send()
        over_tiles(1, sent)
        delivered(1)

    @pl.when(even_chip)
    def _():
        for copy in far_copies:
            copy.wait_send()

    for batch in (0, 2, 3):
        delivered(batch)

    pltpu.make_async_copy(staging, staging, final_recv).wait()
    for half in range(2):
        direct = is_direct(dp, z, r, half)

        @pl.when(direct)
        def _():
            out_ref[pl.ds(half * 128, 128), :] = decode(staging[half])

        @pl.when(jnp.logical_not(direct))
        def _():
            out_ref[pl.ds(half * 128, 128), :] = decode(staging[half]).T


def body(grads):
    dma = pltpu.SemaphoreType.DMA
    return pl.pallas_call(
        kernel,
        out_shape=jax.ShapeDtypeStruct((256, 128), F32),
        in_specs=[pl.BlockSpec(memory_space=pltpu.HBM)],
        out_specs=pl.BlockSpec(memory_space=pltpu.VMEM),
        scratch_shapes=[
            pltpu.VMEM((256, FEATURES), BF16),
            pltpu.VMEM((6, 256, HALF), BF16),
            pltpu.VMEM((TILE_COUNT, 2, 256, 128), F32),
            pltpu.VMEM((TILE_COUNT, 256, 128), F32),
            pltpu.VMEM((TILE_COUNT, 4, 64, 128), F32),
            pltpu.VMEM((3, TILE_COUNT, 64, 128), BF16),
            pltpu.VMEM((3, TILE_COUNT, 64, 128), BF16),
            pltpu.VMEM((4, TILE_COUNT, 16, 128), BF16),
            pltpu.VMEM((4, TILE_COUNT, 16, 128), BF16),
            pltpu.VMEM((TILE_COUNT, 16, 128), BF16),
            pltpu.VMEM((2, 128, 128), BF16),
            pltpu.VMEM((16, 1, 256), F32),
            pltpu.VMEM((2, 1, 128), F32),
            pltpu.VMEM((6, 2, 1, 128), F32),
            pltpu.VMEM((6, 256, 128), F32),
            dma((3, 2, 2)),
            dma((3, 2, 2)),
            dma((2,)),
            dma((2,)),
            dma((2,)),
            dma((3, 2, 2)),
            dma((16,)),
            dma((16,)),
            dma((5, 2)),
            dma((5, 2)),
            dma((TILE_COUNT,)),
            dma((TILE_COUNT,)),
            dma((TILE_COUNT, 4)),
            dma((TILE_COUNT, 4)),
            dma((4, 4)),
            dma((4, 4)),
            dma((TILE_COUNT, 2)),
            dma,
            dma,
            pltpu.SemaphoreType.REGULAR((2,)),
        ],
        compiler_params=pltpu.CompilerParams(
            collective_id=0, has_side_effects=True, vmem_limit_bytes=60 * 1024 * 1024
        ),
        cost_estimate=pl.CostEstimate(flops=1510000000, bytes_accessed=1500000, transcendentals=0),
    )(grads)


def solution(mesh):
    in_specs = (P("dp", "layer"),)
    out_specs = P("dp", ("layer", "rep"))
    return jax.shard_map(body, mesh=mesh, in_specs=in_specs, out_specs=out_specs, check_vma=False)
```

```python
import functools

import jax
import jax.numpy as jnp
from jax import lax
from jax.experimental import pallas as pl
from jax.experimental.pallas import tpu as pltpu
from jax.sharding import PartitionSpec as P

MESH = pl.DeviceIdType.MESH
F32 = jnp.float32
BF16 = jnp.bfloat16
FEATURES = 2560
HALF = FEATURES // 2
CODE_SHIFT = 2.0**-7.5
CODE_SCALE = 13.4
UP, DOWN, OUT, FAR, OWN0, OWN1 = range(6)
TILE_COUNT = 11
BATCHES = ((0, 2), (2, 4), (6, 3), (9, 2))


def edge_bit(h, y):
    return (h + (3 - y % 4) // 3) % 2


def is_direct(dp, layer, rep, half):
    yd, hd = dp // 4, (dp // 2) % 2
    yl, hl = layer // 4, (layer // 2) % 2
    dh, dy = (hl + hd) % 2, (yl - yd + 4) % 4
    parity = (hd + yd + 1) % 2
    mixed = (half + rep) % 2
    above = edge_bit(hd, yd)
    second = edge_bit(hd, yd + 1)
    below = edge_bit(hd, yd + 3)
    same_column = jnp.where(
        dy == 0,
        jnp.where(mixed == 0, 0, half),
        jnp.where(dy == 2, (mixed + above + second + 1) % 2, 1 - parity),
    )
    other_column = jnp.where(
        dy == 1,
        (mixed + above) % 2,
        jnp.where(dy == 3, (mixed + below) % 2, jnp.where(dy == 0, 1 - parity, parity)),
    )
    return jnp.where(dh == 0, same_column, other_column) == 0


def encode(value):
    power = jnp.abs(value) * CODE_SCALE + CODE_SHIFT * CODE_SCALE
    for _ in range(5):
        power = power * power
    return jnp.where(value == 0.0, 0.0, jnp.where(value < 0.0, -power, power)).astype(BF16)


def decode(code):
    wide = code.astype(F32)
    size = jnp.abs(wide)
    root = jnp.maximum(size, 1e-37)
    for _ in range(4):
        root = lax.rsqrt(root)
    value = root * lax.rsqrt(root) * (1.0 / CODE_SCALE) - CODE_SHIFT
    return jnp.where(size < 1e-37, 0.0, jnp.where(wide < 0.0, -value, value))


def kernel(
    grads_ref, out_ref, g_ref, near, part, other, total, pair_code, paired, code, codes, final, staging,
    squares, norm, near_norm, row_scale,
    gather_send, gather_recv, own_send, own_recv, local_sem, far_sem, square_send, square_recv,
    norm_send, norm_recv, core_send, core_recv, pair_send, pair_recv, code_send, code_recv,
    final_send, final_recv, load_sem, entered,
):
    dp = lax.axis_index("dp")
    z = lax.axis_index("layer")
    r = lax.axis_index("rep")
    y, h, c = dp // 4, (dp // 2) % 2, dp % 2
    parity = (h + y + 1) % 2
    g = (r + parity) % 2
    quarter = z % 4
    even_chip = parity == 0
    odd_chip = parity == 1
    last_slot = OUT + 1 - parity

    def device(y_, h_, c_, z_, r_):
        return (4 * ((y_ + 4) % 4) + 2 * (h_ % 2) + c_, (z_ + 16) % 16, r_)

    def remote(src, dst, send, recv, target):
        return pltpu.make_async_remote_copy(
            src_ref=src, dst_ref=dst, send_sem=send, recv_sem=recv, device_id=target, device_id_type=MESH
        )

    load = pltpu.make_async_copy(grads_ref, g_ref, load_sem)
    load.start()

    barrier = pltpu.get_barrier_semaphore()
    partners = [device(y, h, 1 - c, z, r), device(y, h, c, z, 1 - r), device(y + 2, h, c, z, r)]
    partners += [device(y + 1, h + 1, c, z, 1 - r), device(y + 3, h + 1, c, z, 1 - r)]
    for core in range(2):
        partners += [device(y + 1, h, core, z, r), device(y + 3, h, core, z, r), device(y, h + 1, core, z, 1 - r)]
    partners += [device(y, h, c, z + step, r) for step in (-4, -3, -2, -1, 1, 2, 3, 4)]
    for target in partners:
        pl.semaphore_signal(barrier, inc=1, device_id=target, device_id_type=MESH)
    load.wait()
    pl.semaphore_wait(barrier, len(partners))

    wants = (
        (UP, (r + edge_bit(h, y + 3)) % 2, y + 3, h, r),
        (DOWN, (r + edge_bit(h, y)) % 2, y + 1, h, r),
        (OUT, 1 - r, y, h + 1, 1 - r),
    )
    def gather_copies(part_, slot, half, y_, h_, r_):
        rows = pl.ds(pl.multiple_of(half * 128 + part_ * 64, 64), 64)
        return [
            remote(
                g_ref.at[rows, pl.ds(core * HALF, HALF)],
                near.at[slot, pl.ds(pl.multiple_of(c * 128 + part_ * 64, 64), 64)],
                gather_send.at[slot, core, part_],
                gather_recv.at[slot, c, part_],
                device(y_, h_, core, z, r_),
            )
            for core in range(2)
        ]

    gather = [copy for part_ in range(2) for want in wants for copy in gather_copies(part_, *want)]
    for copy in gather:
        copy.start()
    mine = pl.ds(pl.multiple_of(c * HALF, 128), HALF)
    theirs = pl.ds(pl.multiple_of((1 - c) * HALF, 128), HALF)
    place = pl.ds(pl.multiple_of(c * 128, 128), 128)
    own_sends = []
    own_copies = []
    for half in range(2):
        rows = pl.ds(half * 128, 128)
        own_sends.append(
            remote(
                g_ref.at[rows, theirs], near.at[OWN0 + half, place], own_send.at[half], own_recv.at[half],
                device(y, h, 1 - c, z, r),
            )
        )
        own_copies.append(pltpu.make_async_copy(g_ref.at[rows, mine], near.at[OWN0 + half, place], local_sem.at[half]))
    for copy in own_sends + own_copies:
        copy.start()

    @pl.loop(0, 8)
    def _(group):
        wide = g_ref[pl.ds(pl.multiple_of(group * 32, 32), 32), :].astype(F32)
        local = jnp.sum(wide * wide, axis=1, keepdims=True)
        row_scale[0, pl.ds(pl.multiple_of(group * 32, 32), 32)] = jnp.broadcast_to(local, (32, 128))

    squares[z] = row_scale[0].T[0:1, :]
    for step in (-4, 4):
        pl.semaphore_signal(entered, inc=1, device_id=device(y, h, c, z + step, r), device_id_type=MESH)
    pl.semaphore_wait(entered, 2)
    square_sends = []
    for step in range(1, 16):
        square_sends.append(
            remote(
                squares.at[z], squares.at[z], square_send.at[step], square_recv.at[z],
                device(y, h, c, z + step, r),
            )
        )
        square_sends[-1].start()
    def choose(tile, values):
        chosen = values[-1]
        for index in range(len(values) - 2, -1, -1):
            chosen = jnp.where(tile == index, values[index], chosen)
        return chosen

    own = OWN0 + g

    def slots(tile):
        left = choose(tile, (own, OWN0, OWN0, OWN1, OWN0, OWN1, UP, UP, DOWN, OWN0, OWN1))
        right = choose(tile, (own, OWN1, UP, UP, DOWN, DOWN, DOWN, OUT, OUT, last_slot, last_slot))
        return left, right

    def core_copy(tile):
        return remote(
            part.at[tile, 1 - c], other.at[tile], core_send.at[tile], core_recv.at[tile], device(y, h, 1 - c, z, r)
        )

    def over_tiles(batch, step):
        first, count = BATCHES[batch]
        pl.loop(first, first + count)(step)

    def product(tile):
        left, right = slots(tile)
        value = lax.dot_general(near[left], near[right], (((1,), (1,)), ((), ())), preferred_element_type=F32)
        part[tile, 0] = value[:, 0:128]
        part[tile, 1] = value[:, 128:256]
        core_copy(tile).start()

    lanes = (
        (device(y, h, c, z - 1, r), 0, 0, 64),
        (device(y, h, c, z + 1, r), 1, 0, 64),
        (device(y, h, c, z + 2, r), 2, 0, 32),
        (device(y, h, c, z - 2, r), 2, 32, 32),
    )

    def near_copy(lane, tile):
        target, place_, start, size = lanes[lane]
        rows = pl.ds(start, size)
        return remote(
            pair_code.at[place_, tile, rows], paired.at[place_, tile, rows],
            pair_send.at[tile, lane], pair_recv.at[tile, lane], target,
        )

    def join_cores(tile):
        left, right = slots(tile)
        core_copy(tile).wait_recv()
        value = (part[tile, c] + other[tile]) * row_scale[left] * near_norm[right, c]
        total[tile] = value.reshape(4, 64, 128)
        for index, step in enumerate((3, 1, 2)):
            pair_code[index, tile] = encode(total[tile, (quarter + step) % 4])
        for lane in range(4):
            near_copy(lane, tile).start()

    def spread_norms(slot):
        for half in range(2):
            row_scale[slot, pl.ds(128 * half, 128)] = jnp.broadcast_to(near_norm[slot, half], (128, 128)).T

    def encode_tile(tile):
        for lane in range(4):
            near_copy(lane, tile).wait_recv()
        value = total[tile, quarter] + jnp.sum(decode(paired[:, tile]), axis=0)
        coded = encode(value)
        for j in range(4):
            code[j, tile] = coded[16 * j : 16 * j + 16]
        codes[z // 4, tile] = code[z // 4, tile]

    def code_copies(batch):
        first, count = BATCHES[batch]
        copies = []
        for step in range(1, 4):
            slot = (z // 4 + step) % 4
            copies.append(
                remote(
                    code.at[slot, pl.ds(first, count)], codes.at[z // 4, pl.ds(first, count)],
                    code_send.at[batch, step], code_recv.at[batch, z // 4],
                    device(y, h, c, 4 * slot + quarter, r),
                )
            )
        return copies

    def wait_codes(batch):
        first, count = BATCHES[batch]
        for step in range(1, 4):
            slot = (z // 4 + step) % 4
            remote(
                codes.at[slot, pl.ds(first, count)], codes.at[slot, pl.ds(first, count)],
                code_send.at[batch, step], code_recv.at[batch, slot],
                device(y, h, c, 4 * slot + quarter, r),
            ).wait_recv()

    def sum_codes(tile):
        final[tile] = encode(jnp.sum(decode(codes[:, tile]), axis=0))

    row_block = (z % 4) // 2
    offset = pl.multiple_of(64 * (z % 2) + 16 * (z // 4), 16)
    strip = pl.ds(offset, 16)
    far_set = jnp.where(c == 1, (1 - r + edge_bit(h + 1, y + 1 + y % 2)) % 2, r)
    home = 4 * y + 2 * h
    across = 2 - 2 * h
    places = {
        UP: (4 * ((y + 1) % 4) + 2 * h, (r + edge_bit(h, y)) % 2),
        DOWN: (4 * ((y + 3) % 4) + 2 * h, (r + edge_bit(h, y + 3)) % 2),
        OUT: (4 * y + across, r),
        OWN0: (home, 0),
        OWN1: (home, 1),
        "own": (home, g),
        "last": (4 * ((y + 2 - 2 * parity) % 4) + across, jnp.where(even_chip, far_set, r)),
    }
    pairs = (
        ("own", "own"), (OWN0, OWN1), (OWN0, UP), (OWN1, UP), (OWN0, DOWN), (OWN1, DOWN),
        (UP, DOWN), (UP, OUT), (DOWN, OUT), (OWN0, "last"), (OWN1, "last"),
    )
    strips = []
    for tile, (left, right) in enumerate(pairs):
        row, left_set = places[left]
        column, right_set = places[right]
        row, column = row + row_block, column + c
        owner = (row, column, right_set, left_set)
        mirror = (column, row, left_set, right_set)
        if tile == 0:
            targets = (owner,)
        elif tile == 1:
            targets = (tuple(jnp.where(r == 0, a, b) for a, b in zip(owner, mirror)),)
        else:
            targets = (owner, mirror)
        for number, (dp_, z_, r_, half) in enumerate(targets):
            copy = remote(
                final.at[tile], staging.at[half, strip], final_send.at[tile, number], final_recv, (dp_, z_, r_)
            )
            here = None
            if tile < 2 or (number == 0 and left in ("own", OWN0, OWN1)):
                here = jnp.logical_and(jnp.logical_and(dp_ == dp, z_ == z), r_ == r)
            strips.append((tile, copy, here, half))

    def deliver(first, count):
        for tile, copy, here, half in sorted(strips, key=lambda entry: entry[2] is not None):
            if not first <= tile < first + count:
                continue
            if here is None:
                copy.start()
            else:
                pl.when(jnp.logical_not(here))(copy.start)
                pl.when(here)(pltpu.make_async_copy(final.at[tile], staging.at[half, strip], final_recv).start)

    def finish_batch(batch):
        wait_codes(batch)
        first, count = BATCHES[batch]
        for tile in range(first, first + count):
            sum_codes(tile)
        deliver(first, count)

    code_sends = [code_copies(batch) for batch in range(4)]

    def start_codes(batch):
        over_tiles(batch, encode_tile)
        for copy in code_sends[batch]:
            copy.start()

    for half in range(2):
        own_copies[half].wait()
        own_sends[half].wait_recv()
    over_tiles(0, product)

    for step in range(1, 16):
        source = (z + step) % 16
        remote(
            squares.at[source], squares.at[source], square_send.at[step], square_recv.at[source],
            device(y, h, c, z + step, r),
        ).wait_recv()
    inverse = lax.rsqrt(jnp.sum(squares[...], axis=0) + 1e-06)
    norm[0] = inverse[:, 0:128]
    norm[1] = inverse[:, 128:256]
    norm_sends = []
    for slot, half, y_, h_, r_ in wants:
        for core in range(2):
            norm_sends.append(
                remote(
                    norm.at[half], near_norm.at[slot, c], norm_send.at[slot, core], norm_recv.at[slot, c],
                    device(y_, h_, core, z, r_),
                )
            )
    for half in range(2):
        near_norm[OWN0 + half, c] = norm[half]
        norm_sends.append(
            remote(
                norm.at[half], near_norm.at[OWN0 + half, c], norm_send.at[4, half], norm_recv.at[4, half],
                device(y, h, 1 - c, z, r),
            )
        )
    for copy in norm_sends:
        copy.start()

    for half in range(2):
        remote(
            near_norm.at[OWN0 + half, 1 - c], near_norm.at[OWN0 + half, 1 - c], norm_send.at[4, half], norm_recv.at[4, half],
            device(y, h, 1 - c, z, r),
        ).wait_recv()
    for slot in (OWN0, OWN1):
        spread_norms(slot)
    over_tiles(0, join_cores)

    def norm_arrived(slot):
        for core in range(2):
            remote(
                near_norm.at[slot, core], near_norm.at[slot, core],
                norm_send.at[slot, core], norm_recv.at[slot, core], device(y, h, 1 - c, z, r),
            ).wait_recv()

    def arrived(slot, core, part_):
        rows = pl.ds(core * 128 + part_ * 64, 64)
        remote(
            near.at[slot, rows], near.at[slot, rows],
            gather_send.at[slot, core, part_], gather_recv.at[slot, core, part_], device(y, h, 1 - c, z, r),
        ).wait_recv()

    for slot in (UP, DOWN, OUT):
        norm_arrived(slot)
    for slot in (UP, DOWN):
        spread_norms(slot)

    far_copies = []

    def forward(number, part_):
        slot, target = (
            (OUT, device(y + 2, h, c, z, r)), (DOWN - y % 2, device(y + 1 + 2 * (y % 2), h + 1, c, z, 1 - r))
        )[number]
        arrived(slot, number, part_)
        rows = pl.ds(128 * number + 64 * part_, 64)
        copies = [
            remote(
                near.at[slot, rows], near.at[FAR, rows],
                far_sem.at[0, number, part_], far_sem.at[1, number, part_], target,
            )
        ]
        if part_ == 0:
            copies.append(
                remote(
                    near_norm.at[slot, number], near_norm.at[FAR, number],
                    far_sem.at[2, number, 0], far_sem.at[2, number, 1], target,
                )
            )

        @pl.when(even_chip)
        def _():
            for copy in copies:
                copy.start()

        far_copies.extend(copies)

    start_codes(0)

    for part_ in range(2):
        forward(0, part_)
        forward(1, part_)
    for part_ in range(2):
        arrived(OUT, 1, part_)
        arrived(DOWN - y % 2, 0, part_)
        for core in range(2):
            arrived(UP + y % 2, core, part_)

    @pl.when(odd_chip)
    def _():
        over_tiles(1, product)
        over_tiles(3, product)
        over_tiles(1, join_cores)
        over_tiles(2, product)
        over_tiles(3, join_cores)
        over_tiles(2, join_cores)
        start_codes(1)
        start_codes(3)
        start_codes(2)
        finish_batch(0)
        finish_batch(1)
        finish_batch(3)
        finish_batch(2)

    @pl.when(even_chip)
    def _():
        over_tiles(2, product)
        over_tiles(2, join_cores)
        start_codes(2)
        finish_batch(0)
        for copy in far_copies:
            copy.wait_recv()
        over_tiles(3, product)
        over_tiles(3, join_cores)
        start_codes(3)
        finish_batch(2)
        finish_batch(3)

    waits = gather + square_sends + own_sends + norm_sends
    for batch in (0, 2, 3):
        waits += code_sends[batch]
    for copy in waits:
        copy.wait_send()

    def sent(tile):
        core_copy(tile).wait_send()
        for lane in range(4):
            near_copy(lane, tile).wait_send()

    def delivered(batch):
        first, count = BATCHES[batch]
        for tile, copy, here, _ in strips:
            if not first <= tile < first + count:
                continue
            if here is None:
                copy.wait_send()
            else:
                pl.when(jnp.logical_not(here))(copy.wait_send)

    for batch in (0, 2, 3):
        over_tiles(batch, sent)

    @pl.when(odd_chip)
    def _():
        for copy in code_sends[1]:
            copy.wait_send()
        over_tiles(1, sent)
        delivered(1)

    @pl.when(even_chip)
    def _():
        for copy in far_copies:
            copy.wait_send()

    for batch in (0, 2, 3):
        delivered(batch)

    pltpu.make_async_copy(staging, staging, final_recv).wait()
    for half in range(2):
        direct = is_direct(dp, z, r, half)

        @pl.when(direct)
        def _():
            out_ref[pl.ds(half * 128, 128), :] = decode(staging[half])

        @pl.when(jnp.logical_not(direct))
        def _():
            out_ref[pl.ds(half * 128, 128), :] = decode(staging[half]).T


def body(grads):
    dma = pltpu.SemaphoreType.DMA
    return pl.pallas_call(
        kernel,
        out_shape=jax.ShapeDtypeStruct((256, 128), F32),
        in_specs=[pl.BlockSpec(memory_space=pltpu.HBM)],
        out_specs=pl.BlockSpec(memory_space=pltpu.VMEM),
        scratch_shapes=[
            pltpu.VMEM((256, FEATURES), BF16),
            pltpu.VMEM((6, 256, HALF), BF16),
            pltpu.VMEM((TILE_COUNT, 2, 256, 128), F32),
            pltpu.VMEM((TILE_COUNT, 256, 128), F32),
            pltpu.VMEM((TILE_COUNT, 4, 64, 128), F32),
            pltpu.VMEM((3, TILE_COUNT, 64, 128), BF16),
            pltpu.VMEM((3, TILE_COUNT, 64, 128), BF16),
            pltpu.VMEM((4, TILE_COUNT, 16, 128), BF16),
            pltpu.VMEM((4, TILE_COUNT, 16, 128), BF16),
            pltpu.VMEM((TILE_COUNT, 16, 128), BF16),
            pltpu.VMEM((2, 128, 128), BF16),
            pltpu.VMEM((16, 1, 256), F32),
            pltpu.VMEM((2, 1, 128), F32),
            pltpu.VMEM((6, 2, 1, 128), F32),
            pltpu.VMEM((6, 256, 128), F32),
            dma((3, 2, 2)),
            dma((3, 2, 2)),
            dma((2,)),
            dma((2,)),
            dma((2,)),
            dma((3, 2, 2)),
            dma((16,)),
            dma((16,)),
            dma((5, 2)),
            dma((5, 2)),
            dma((TILE_COUNT,)),
            dma((TILE_COUNT,)),
            dma((TILE_COUNT, 4)),
            dma((TILE_COUNT, 4)),
            dma((4, 4)),
            dma((4, 4)),
            dma((TILE_COUNT, 2)),
            dma,
            dma,
            pltpu.SemaphoreType.REGULAR,
        ],
        compiler_params=pltpu.CompilerParams(
            collective_id=0, has_side_effects=True, vmem_limit_bytes=60 * 1024 * 1024
        ),
        cost_estimate=pl.CostEstimate(flops=1510000000, bytes_accessed=1500000, transcendentals=0),
    )(grads)


def solution(mesh):
    in_specs = (P("dp", "layer"),)
    out_specs = P("dp", ("layer", "rep"))
    return jax.shard_map(body, mesh=mesh, in_specs=in_specs, out_specs=out_specs, check_vma=False)
```
